512 devices in a mesh: kvh: 8 (over x, core), seq: 64 (over z, y).
Axes of the slice: x: 4, y: 8, z: 8, core: 2. Of those that a mesh axis runs over, the one named last changes fastest.
Arguments:
- queries: bfloat16 [4, 4, 16384], P(None, None, ('kvh', 'seq')), may hold values from -60 to 60
- drafted_key_value: bfloat16 [4, 4, 2, 8, 128], P(None, None, None, 'kvh'), may hold values from -6 to 6
- paged_key_value: bfloat16 [2, 8, 512, 128, 128], P(None, 'kvh', 'seq'), may hold values from -6 to 6
- block_table: int32 [4, 128], replicated, may hold values from -1 to 511, as said below
- page_count: int32 [4], replicated, may hold values from 1 to 128
- tail_fill: int32 [4], replicated, may hold values from 1 to 128
- out_weight: bfloat16 [16384, 16384], P('kvh', 'seq'), may hold values from -0.375 to 0.375
- stream_in: float32 [4, 4, 16384], P(None, None, 'seq'), may hold values from -4 to 4
- norm_gain: float32 [16384], P('seq'), may hold values from 0.1 to 1.9
- gate_up: bfloat16 [2, 26624, 16384], P(None, ('kvh', 'seq')), may hold values from -0.046875 to 0.046875
Outputs:
- hidden: bfloat16 [4, 4, 26624], P(None, None, ('kvh', 'seq'))
- stream: float32 [4, 4, 16384], P(None, None, 'seq')
The draws below stay inside these ranges and needn't reach their ends.
Inputs may be any that keep to these rules, and one draw needn't show every extreme that they name: `block_table`: each slot stands at most once in the table; entries at pages from page_count on are -1, the others are slots.
All inputs are finite; a program needn't handle non-finite values.
Results may differ from the reference program's by a relative error of at most 0.0095.
Values may be sent and summed in bfloat16 or wider, within the bound.
No kernel may reach another device: no remote copies, remote signals or barrier semaphores. Data moves between devices by JAX's collectives and lax.ppermute only.
A program may use at most 64 MiB of HBM per device.

```python
import jax
import jax.numpy as jnp
from jax import lax

D = 16384
QUERY_HEADS = 128
KEY_VALUE_HEADS = 8
HEAD_SIZE = 128
FFW = 26624
DRAFT_STEPS = 4
PAGE_TOKENS = 128
SEQUENCE_ROWS = 4
PAGES_DEV = 8
PAGE_SLOTS = 512
MOST_PAGES = 128


def page_layout(key):
    count_key, top_key, spread_key, noise_key = jax.random.split(key, 4)
    counts = jax.random.randint(count_key, (SEQUENCE_ROWS,), 1, MOST_PAGES + 1)
    top = jax.random.randint(top_key, (), 0, SEQUENCE_ROWS)
    counts = jnp.where(jnp.arange(SEQUENCE_ROWS) == top, MOST_PAGES, counts).astype(jnp.int32)
    spread = jax.random.randint(spread_key, (PAGE_SLOTS // PAGES_DEV, 1), 1, 5)
    level = (jnp.arange(PAGES_DEV)[None, :] * spread).reshape(PAGE_SLOTS)
    noise = jax.random.randint(noise_key, (PAGE_SLOTS,), 0, PAGE_SLOTS)
    order = jnp.argsort(level * PAGE_SLOTS + noise, stable=True).astype(jnp.int32)
    offset = jnp.cumsum(counts) - counts
    pages = jnp.arange(MOST_PAGES)
    position = jnp.minimum(offset[:, None] + pages[None, :], PAGE_SLOTS - 1)
    table = jnp.where(pages[None, :] < counts[:, None], order[position], -1)
    return (counts, table.astype(jnp.int32))


def draw_page_count(key, part):
    counts, table = page_layout(key)
    return counts


def draw_block_table(key, part):
    counts, table = page_layout(key)
    return table


def draw_queries(key, part):
    key = jax.random.fold_in(key, 11)
    base_key = jax.random.fold_in(key, 0)
    base = jax.random.normal(base_key, (DRAFT_STEPS, SEQUENCE_ROWS, QUERY_HEADS * HEAD_SIZE), jnp.float32)
    return jnp.clip(base, -6.0, 6.0).astype(jnp.bfloat16)


def set_ends(drawn, key, low, high):
    index_at = [jax.random.randint(jax.random.fold_in(key, axis), (), 0, length) for axis, length in enumerate(drawn.shape)]
    main_axis = drawn.shape.index(max(drawn.shape))
    next_to = index_at[:main_axis] + [(index_at[main_axis] + 1) % drawn.shape[main_axis]] + index_at[main_axis + 1:]
    return drawn.at[tuple(index_at)].set(low).at[tuple(next_to)].set(high)


def levels(key, shape, cuts, low, largest):
    factor_of, own = 1.0, jax.random.fold_in(key, 6)
    for axis_at, blocks in cuts:
        draws = jnp.exp(jax.random.uniform(jax.random.fold_in(own, axis_at), (blocks,), jnp.float32, low / len(cuts), largest / len(cuts)))
        factor_of = factor_of * jnp.repeat(draws, shape[axis_at] // blocks).reshape([-1 if axis == axis_at else 1 for axis in range(len(shape))])
    return factor_of


def bell_draw(key, shape, deviation, most, shards=(), kind=jnp.bfloat16):
    drawn = jax.random.normal(key, shape, jnp.float32) * deviation
    if len(shards) > 0:
        drawn = levels(key, shape, shards, -0.22, 0.18) * drawn
    return jnp.clip(drawn, min=-most, max=most).astype(kind)


def setup_inputs(seed: int = 0) -> dict:
    arg_keys = jax.random.split(jax.random.key(seed), 11)
    queries = draw_queries(jax.random.fold_in(arg_keys[10], 71), 0)
    drafted_key_value = bell_draw(arg_keys[1], (DRAFT_STEPS, SEQUENCE_ROWS, 2, KEY_VALUE_HEADS, HEAD_SIZE), 1.0, 6.0, ((3, 8),))
    paged_key_value = bell_draw(arg_keys[2], (2, KEY_VALUE_HEADS, PAGE_SLOTS, PAGE_TOKENS, HEAD_SIZE), 1.0, 6.0, ((1, 8), (2, 64)))
    block_table = draw_block_table(jax.random.fold_in(arg_keys[10], 71), 0)
    page_count = draw_page_count(jax.random.fold_in(arg_keys[10], 71), 0)
    tail_fill = set_ends(jax.random.randint(arg_keys[5], (SEQUENCE_ROWS,), 1, PAGE_TOKENS + 1), jax.random.fold_in(arg_keys[5], 1), 1, PAGE_TOKENS).astype(jnp.int32)
    out_weight = bell_draw(arg_keys[6], (QUERY_HEADS * HEAD_SIZE, D), (QUERY_HEADS * HEAD_SIZE // 64) ** -0.5, 0.375, ((0, 8), (1, 64)))
    stream_in = bell_draw(arg_keys[7], (DRAFT_STEPS, SEQUENCE_ROWS, D), 0.5, 4.0, ((2, 64),), jnp.float32)
    norm_gain = jnp.clip(1.0 + 0.18 * jax.random.normal(arg_keys[8], (D,), jnp.float32), 0.1, 1.9)
    gate_up = bell_draw(arg_keys[9], (2, FFW, D), D ** -0.5, 0.046875, ((1, 512),))
    return {"queries": queries, "drafted_key_value": drafted_key_value, "paged_key_value": paged_key_value, "block_table": block_table, "page_count": page_count, "tail_fill": tail_fill, "out_weight": out_weight, "stream_in": stream_in, "norm_gain": norm_gain, "gate_up": gate_up}


big_negative = -1e+30
epsilon = 1e-05

def reference(queries, drafted_key_value, paged_key_value, block_table, page_count, tail_fill, out_weight, stream_in, norm_gain, gate_up):
    query_group = QUERY_HEADS // KEY_VALUE_HEADS
    scale = HEAD_SIZE ** (-0.5)
    query_matrix = jnp.transpose(queries.reshape(DRAFT_STEPS, SEQUENCE_ROWS, KEY_VALUE_HEADS, query_group, HEAD_SIZE), (1, 0, 2, 3, 4)).astype(jnp.float32)
    fresh_rows = jnp.transpose(drafted_key_value, (1, 0, 2, 3, 4)).astype(jnp.float32)
    page_index = jnp.arange(MOST_PAGES, dtype=jnp.int32)
    token_index = jnp.arange(PAGE_TOKENS, dtype=jnp.int32)
    causal = jnp.arange(DRAFT_STEPS)[None, :] <= jnp.arange(DRAFT_STEPS)[:, None]

    def one_row(items):
        query_row, table_row, count, tail, fresh_row = items
        guarded_mask = jnp.maximum(table_row, 0)
        key_rows = paged_key_value[0][:, guarded_mask].astype(jnp.float32).reshape(KEY_VALUE_HEADS, MOST_PAGES * PAGE_TOKENS, HEAD_SIZE)
        value_rows = paged_key_value[1][:, guarded_mask].astype(jnp.float32).reshape(KEY_VALUE_HEADS, MOST_PAGES * PAGE_TOKENS, HEAD_SIZE)
        valid = (page_index[:, None] < count - 1) | (page_index[:, None] == count - 1) & (token_index[None, :] < tail)
        valid = valid.reshape(MOST_PAGES * PAGE_TOKENS)
        cache_scores = jnp.einsum('shgd,hkd->shgk', query_row, key_rows, precision=lax.Precision.HIGHEST) * scale
        cache_scores = jnp.where(valid[None, None, None, :], cache_scores, big_negative)
        fresh_scores = jnp.einsum('shgd,uhd->shgu', query_row, fresh_row[:, 0], precision=lax.Precision.HIGHEST) * scale
        fresh_ok = causal[:, None, None, :]
        fresh_scores = jnp.where(fresh_ok, fresh_scores, big_negative)
        peak = jnp.maximum(lax.optimization_barrier(jnp.max(cache_scores, axis=3)), lax.optimization_barrier(jnp.max(fresh_scores, axis=3)))
        cache_weights = jnp.where(valid[None, None, None, :], jnp.exp(cache_scores - peak[..., None]), 0.0)
        fresh_weights = jnp.where(fresh_ok, jnp.exp(fresh_scores - peak[..., None]), 0.0)
        total = lax.optimization_barrier(jnp.sum(cache_weights, axis=3)) + lax.optimization_barrier(jnp.sum(fresh_weights, axis=3))
        summed = jnp.einsum('shgk,hkd->shgd', cache_weights, value_rows, precision=lax.Precision.HIGHEST)
        summed = summed + jnp.einsum('shgu,uhd->shgd', fresh_weights, fresh_row[:, 1], precision=lax.Precision.HIGHEST)
        return summed / total[..., None]
    outputs = lax.map(one_row, (query_matrix, block_table, page_count, tail_fill, fresh_rows))
    attended = jnp.transpose(outputs, (1, 0, 2, 3, 4)).reshape(DRAFT_STEPS * SEQUENCE_ROWS, QUERY_HEADS * HEAD_SIZE).astype(jnp.bfloat16)
    projected = jnp.dot(attended, out_weight, preferred_element_type=jnp.float32)
    stream = stream_in.reshape(DRAFT_STEPS * SEQUENCE_ROWS, D) + projected
    mean_square = lax.optimization_barrier(jnp.mean(stream * stream, axis=1))
    inverse = lax.rsqrt(mean_square + epsilon)
    scaled = (stream * norm_gain[None, :]).astype(jnp.bfloat16)
    gate = jnp.dot(scaled, gate_up[0].T, preferred_element_type=jnp.float32) * inverse[:, None]
    up_part = jnp.dot(scaled, gate_up[1].T, preferred_element_type=jnp.float32) * inverse[:, None]
    hidden = (jax.nn.silu(gate) * up_part).astype(jnp.bfloat16)
    return (hidden.reshape(DRAFT_STEPS, SEQUENCE_ROWS, FFW), stream.reshape(DRAFT_STEPS, SEQUENCE_ROWS, D))
```

```python
import jax
import jax.numpy as jnp
from jax import lax
from jax.experimental import pallas as pl
from jax.experimental.pallas import tpu as pltpu
from jax.sharding import Mesh
from jax.sharding import PartitionSpec as P

QUERY_HEADS = 128
KEY_VALUE_HEADS = 8
GROUP = QUERY_HEADS // KEY_VALUE_HEADS
WIDTH = 128
STEPS = 4
ROWS = 4
COUNT = STEPS * ROWS
QUARTER = 32
SIDE = 8

low = -1e30
floor = -1e29
epsilon = 1e-05
f32 = jnp.float32
bf16 = jnp.bfloat16


def iota(shape, axis):
    return lax.broadcasted_iota(jnp.int32, shape, axis)


def dot(a, b):
    return lax.dot_general(a, b, (((1,), (0,)), ((), ())), preferred_element_type=f32)


def dot_t(a, b):
    return lax.dot_general(a, b, (((1,), (1,)), ((), ())), preferred_element_type=f32)


def split(x):
    hi = x.astype(bf16).astype(f32)
    return hi, x - hi


def call(body, out_shape, scratch=(), limit=32 * 2**20, cost=None):
    return pl.pallas_call(
        body,
        out_shape=out_shape,
        scratch_shapes=list(scratch),
        compiler_params=pltpu.CompilerParams(vmem_limit_bytes=limit),
    )


def attend(gathered, paged, fresh_keys, fresh_values, bias, fresh_bias, out, block):
    sent = jnp.concatenate([gathered[:, i, :].astype(f32) for i in range(STEPS)], axis=0)
    shape = (STEPS * GROUP * 4, WIDTH)
    quarter = iota(shape, 0) % 4
    diagonal = iota(shape, 1) // QUARTER == quarter
    turned = [sent] + [pltpu.roll(sent, QUARTER * d, 1) for d in range(1, 4)]
    pick_row = iota((GROUP * STEPS, shape[0]), 0)
    pick_col = iota((GROUP * STEPS, shape[0]), 1)
    pick = (pick_row // STEPS == (pick_col // 4) % GROUP) & (
        pick_row % STEPS == pick_col // (4 * GROUP)
    )
    pick = jnp.where(pick, 1.0, 0.0).astype(bf16)
    keys = paged[0, 0].reshape(-1, WIDTH)
    values = paged[1, 0].reshape(-1, WIDTH)
    fresh_k = fresh_keys[...]
    fresh_v = fresh_values[...]
    ones = jnp.ones((keys.shape[0], WIDTH), bf16)
    fresh_ones = jnp.ones((fresh_k.shape[0], WIDTH), bf16)
    scale = WIDTH ** (-0.5)
    lane = iota((GROUP * STEPS, WIDTH), 1)
    place = iota((GROUP * STEPS, WIDTH), 0) % 8
    stats = None
    for r in range(ROWS):
        chosen = turned[(3 - r) % 4]
        for c in range(3):
            chosen = jnp.where(quarter == c, turned[(c - r) % 4], chosen)
        chosen = jnp.where(diagonal, chosen, 0.0).astype(bf16)
        query = dot(pick, chosen).astype(bf16)
        scores = dot_t(query, keys) * scale + bias[r : r + 1, :]
        fresh = dot_t(query, fresh_k) * scale + fresh_bias[r]
        peak = jnp.maximum(
            jnp.max(scores, axis=1, keepdims=True), jnp.max(fresh, axis=1, keepdims=True)
        )
        peak = jnp.maximum(peak, floor).astype(bf16).astype(f32)
        weights = jnp.exp(scores - peak).astype(bf16)
        fresh_weights = jnp.exp(fresh - peak).astype(bf16)
        total = dot(weights, ones) + dot(fresh_weights, fresh_ones)
        summed = dot(weights, values) + dot(fresh_weights, fresh_v)
        mean = summed / jnp.where(total > 0.0, total, 1.0)
        block[:, 8 * r : 8 * r + 8, :] = mean.reshape(SIDE, 8, WIDTH)
        hi, rest = split(total)
        at = lane - place - 8 * r
        stat = jnp.where(at == 0, peak, jnp.where(at == 32, hi, jnp.where(at == 64, rest, 0.0)))
        stats = stat if stats is None else stats + stat
    stats = stats.reshape(SIDE, 8, WIDTH)
    block[:, 32:40, :] = jnp.broadcast_to(
        jnp.sum(stats, axis=1, keepdims=True), (SIDE, 8, WIDTH)
    )
    out[...] = block[...].astype(bf16)


def merged(got):
    parts = got[...].astype(f32)
    n = parts.shape[0]
    means, stats = parts[:, :32, :], parts[:, 32:40, :]
    stats = jnp.concatenate([stats] * 4, axis=1).reshape(n * 32, WIDTH)
    at = iota((n * 32, WIDTH), 1) - iota((n * 32, WIDTH), 0) % 32
    ones = jnp.ones((WIDTH, WIDTH), bf16)
    peaks = dot(jnp.where(at == 0, stats, 0.0).astype(bf16), ones).reshape(n, 32, WIDTH)
    totals = dot(jnp.where((at == 32) | (at == 64), stats, 0.0).astype(bf16), ones)
    totals = totals.reshape(n, 32, WIDTH)
    peak = jnp.max(peaks, axis=0)
    factors = jnp.exp(peaks - peak[None]) * totals
    total = jnp.sum(factors, axis=0)
    mean = jnp.sum(factors * means, axis=0) / jnp.where(total > 0.0, total, 1.0)
    return peak, total, mean


def join(got, out):
    peak, total, mean = merged(got)
    hi, rest = split(total)
    at = iota((32, WIDTH), 1) - iota((32, WIDTH), 0)
    stat = jnp.where(at == 0, peak, jnp.where(at == 32, hi, jnp.where(at == 64, rest, 0.0)))
    stat = jnp.broadcast_to(jnp.sum(stat, axis=0, keepdims=True), (8, WIDTH))
    block = jnp.concatenate([mean, stat], axis=0).astype(bf16)
    out[...] = jnp.broadcast_to(block[None], out.shape)


def finish(got, out):
    peak, total, mean = merged(got)
    to, of = iota((32, 32), 0), iota((32, 32), 1)
    move = (to // 16 == (of // 4) % 2) & ((to // 4) % 4 == of % 4) & (to % 4 == of // 8)
    moved = dot(jnp.where(move, 1.0, 0.0).astype(bf16), mean.astype(bf16)).astype(bf16)
    out[...] = jnp.broadcast_to(moved[None], out.shape)


def project(attended, weight, out):
    features = jnp.concatenate(
        [attended[i, COUNT * j : COUNT * (j + 1), :] for i in range(SIDE) for j in range(2)],
        axis=1,
    )
    out[...] = jnp.broadcast_to(dot(features, weight[...])[None], out.shape)


def normalise(parts, stream_in, gain, out, stream_out):
    stream = stream_in[...] + jnp.sum(parts[...], axis=0)
    for i in range(STEPS):
        stream_out[i] = stream[ROWS * i : ROWS * (i + 1)]
    squares = jnp.sum(stream * stream, axis=1, keepdims=True)
    hi, rest = split(squares)
    mid, rest = split(rest)
    at = iota((COUNT, WIDTH), 1) - iota((COUNT, WIDTH), 0)
    stat = jnp.where(at == 0, hi, jnp.where(at == 32, mid, jnp.where(at == 64, rest, 0.0)))
    stat = jnp.broadcast_to(jnp.sum(stat, axis=0, keepdims=True), (8, WIDTH))
    scaled = stream * gain[...]
    block = jnp.concatenate([scaled[:, :WIDTH], scaled[:, WIDTH:], stat], axis=0).astype(bf16)
    out[...] = jnp.broadcast_to(block[None], out.shape)


def feed(got, weight, out):
    n = got.shape[0]
    tokens = jnp.concatenate(
        [got[s, COUNT * j : COUNT * (j + 1), :] for s in range(n) for j in range(2)], axis=1
    )
    stats = jnp.sum(got[:, 32:40, :].astype(f32), axis=0)
    stats = jnp.concatenate([stats, stats], axis=0)
    at = iota((COUNT, WIDTH), 1) - iota((COUNT, WIDTH), 0)
    stats = jnp.where((at == 0) | (at == 32) | (at == 64), stats, 0.0)
    squares = jnp.sum(stats, axis=1, keepdims=True)
    inverse = lax.rsqrt(squares / (n * 2 * WIDTH) + epsilon)
    gate = dot_t(tokens, weight[0]) * inverse
    up = dot_t(tokens, weight[1]) * inverse
    hidden = gate / (1.0 + jnp.exp(-gate)) * up
    for i in range(STEPS):
        out[i] = hidden[ROWS * i : ROWS * (i + 1)].astype(bf16)


def send(x, axis):
    return lax.all_to_all(x, axis, split_axis=0, concat_axis=0, tiled=True)


def shards(
    queries,
    drafted_key_value,
    paged_key_value,
    block_table,
    page_count,
    tail_fill,
    out_weight,
    stream_in,
    norm_gain,
    gate_up,
):
    seq_index = lax.axis_index(("z", "y"))
    seq_count = lax.axis_size(("z", "y"))
    pages, page_len = paged_key_value.shape[2], paged_key_value.shape[3]
    columns = out_weight.shape[1]
    units = gate_up.shape[1]

    mine = queries.reshape(STEPS, ROWS * QUARTER)
    gathered = send(jnp.broadcast_to(mine[None], (seq_count, *mine.shape)), ("z", "y"))

    slots = seq_index * pages + jnp.arange(pages, dtype=jnp.int32)
    page_index = jnp.arange(block_table.shape[1], dtype=jnp.int32)
    held = (block_table[:, :, None] == slots[None, None, :]) & (
        page_index[None, :, None] < page_count[:, None, None]
    )
    last = page_index[None, :] == page_count[:, None] - 1
    fill = jnp.where(last, tail_fill[:, None], page_len)
    filled = jnp.max(jnp.where(held, fill[:, :, None], 0), axis=1)
    bias = jnp.where(jnp.arange(page_len)[None, None, :] < filled[:, :, None], 0.0, low)
    bias = bias.reshape(ROWS, pages * page_len).astype(f32)
    row = jnp.arange(ROWS)[:, None, None]
    step = (jnp.arange(GROUP * STEPS) % STEPS)[None, :, None]
    key = jnp.arange(COUNT)[None, None, :]
    ok = (key % ROWS == row) & (key // ROWS <= step) & (row == seq_index)
    fresh_bias = jnp.where(ok, 0.0, low).astype(f32)
    fresh_keys = drafted_key_value[:, :, 0, 0].reshape(COUNT, WIDTH)
    fresh_values = drafted_key_value[:, :, 1, 0].reshape(COUNT, WIDTH)

    shape = jax.ShapeDtypeStruct
    block = call(
        attend, shape((SIDE, 40, WIDTH), bf16), [pltpu.VMEM((SIDE, 40, WIDTH), f32)]
    )(gathered, paged_key_value, fresh_keys, fresh_values, bias, fresh_bias)
    block = call(join, shape((SIDE, 40, WIDTH), bf16))(send(block, "y"))
    attended = call(finish, shape((SIDE, 32, WIDTH), bf16))(send(block, "z"))
    partial_sum = call(project, shape((SIDE, COUNT, columns), f32))(
        send(attended, "y"), out_weight
    )
    scaled, stream = call(
        normalise,
        (shape((SIDE, 40, WIDTH), bf16), shape((STEPS, ROWS, columns), f32)),
    )(
        send(partial_sum, ("x", "core")),
        stream_in.reshape(COUNT, columns),
        norm_gain.reshape(1, columns),
    )
    scaled = lax.all_gather(send(scaled, "y"), "z").reshape(seq_count, 40, WIDTH)
    hidden = call(feed, shape((STEPS, ROWS, units), bf16))(scaled, gate_up)
    return hidden, stream


def solution(mesh):
    fine = Mesh(mesh.devices.reshape(4, 2, 8, 8), ("x", "core", "z", "y"))
    kvh, seq = ("x", "core"), ("z", "y")
    placed = (
        P(None, None, kvh + seq),
        P(None, None, None, kvh, None),
        P(None, kvh, seq, None, None),
        P(),
        P(),
        P(),
        P(kvh, seq),
        P(None, None, seq),
        P(seq),
        P(None, kvh + seq, None),
    )
    return jax.shard_map(
        shards,
        mesh=fine,
        in_specs=placed,
        out_specs=(P(None, None, kvh + seq), P(None, None, seq)),
        check_vma=False,
    )
```

```python
import jax
import jax.numpy as jnp
from jax import lax
from jax.experimental import pallas as pl
from jax.experimental.pallas import tpu as pltpu
from jax.sharding import Mesh
from jax.sharding import PartitionSpec as P

QUERY_HEADS = 128
KEY_VALUE_HEADS = 8
GROUP = QUERY_HEADS // KEY_VALUE_HEADS
WIDTH = 128
STEPS = 4
ROWS = 4
COUNT = STEPS * ROWS
QUARTER = 32
SIDE = 8

low = -1e30
floor = -1e29
epsilon = 1e-05
f32 = jnp.float32
bf16 = jnp.bfloat16


def iota(shape, axis):
    return lax.broadcasted_iota(jnp.int32, shape, axis)


def dot(a, b):
    return lax.dot_general(a, b, (((1,), (0,)), ((), ())), preferred_element_type=f32)


def dot_t(a, b):
    return lax.dot_general(a, b, (((1,), (1,)), ((), ())), preferred_element_type=f32)


def split(x):
    hi = x.astype(bf16).astype(f32)
    return hi, x - hi


def call(body, out_shape, scratch=(), limit=32 * 2**20, cost=None):
    return pl.pallas_call(
        body,
        out_shape=out_shape,
        scratch_shapes=list(scratch),
        compiler_params=pltpu.CompilerParams(vmem_limit_bytes=limit),
    )


def copies(queries, out):
    x = queries[...].astype(f32)
    x = jnp.concatenate([x[:, r, :] for r in range(ROWS)], axis=1).astype(bf16)
    out[...] = jnp.broadcast_to(x[None], out.shape)


def fetch(*refs):
    n = len(refs) // 2
    moves = [pltpu.make_async_copy(refs[i], refs[n + i], refs[-1].at[i]) for i in range(n)]
    for move in moves:
        move.start()
    for move in moves:
        move.wait()


def attend(gathered, paged, fresh_keys, fresh_values, bias, fresh_bias, out, block):
    sent = jnp.concatenate([gathered[:, i, :].astype(f32) for i in range(STEPS)], axis=0)
    shape = (STEPS * GROUP * 4, WIDTH)
    quarter = iota(shape, 0) % 4
    diagonal = iota(shape, 1) // QUARTER == quarter
    turned = [sent] + [pltpu.roll(sent, QUARTER * d, 1) for d in range(1, 4)]
    pick_row = iota((GROUP * STEPS, shape[0]), 0)
    pick_col = iota((GROUP * STEPS, shape[0]), 1)
    pick = (pick_row // STEPS == (pick_col // 4) % GROUP) & (
        pick_row % STEPS == pick_col // (4 * GROUP)
    )
    pick = jnp.where(pick, 1.0, 0.0).astype(bf16)
    keys = paged[0, 0].reshape(-1, WIDTH)
    values = paged[1, 0].reshape(-1, WIDTH)
    fresh_k = fresh_keys[...]
    fresh_v = fresh_values[...]
    ones = jnp.ones((keys.shape[0], WIDTH), bf16)
    fresh_ones = jnp.ones((fresh_k.shape[0], WIDTH), bf16)
    scale = WIDTH ** (-0.5)
    lane = iota((GROUP * STEPS, WIDTH), 1)
    place = iota((GROUP * STEPS, WIDTH), 0) % 8
    stats = None
    for r in range(ROWS):
        chosen = turned[(3 - r) % 4]
        for c in range(3):
            chosen = jnp.where(quarter == c, turned[(c - r) % 4], chosen)
        chosen = jnp.where(diagonal, chosen, 0.0).astype(bf16)
        query = dot(pick, chosen).astype(bf16)
        scores = dot_t(query, keys) * scale + bias[r : r + 1, :]
        fresh = dot_t(query, fresh_k) * scale + fresh_bias[r]
        peak = jnp.maximum(
            jnp.max(scores, axis=1, keepdims=True), jnp.max(fresh, axis=1, keepdims=True)
        )
        peak = jnp.maximum(peak, floor).astype(bf16).astype(f32)
        weights = jnp.exp(scores - peak).astype(bf16)
        fresh_weights = jnp.exp(fresh - peak).astype(bf16)
        total = dot(weights, ones) + dot(fresh_weights, fresh_ones)
        summed = dot(weights, values) + dot(fresh_weights, fresh_v)
        mean = summed / jnp.where(total > 0.0, total, 1.0)
        block[:, 8 * r : 8 * r + 8, :] = mean.reshape(SIDE, 8, WIDTH)
        hi, rest = split(total)
        at = lane - place - 8 * r
        stat = jnp.where(at == 0, peak, jnp.where(at == 32, hi, jnp.where(at == 64, rest, 0.0)))
        stats = stat if stats is None else stats + stat
    stats = stats.reshape(SIDE, 8, WIDTH)
    block[:, 32:40, :] = jnp.broadcast_to(
        jnp.sum(stats, axis=1, keepdims=True), (SIDE, 8, WIDTH)
    )
    out[...] = block[...].astype(bf16)


def merged(got):
    parts = got[...].astype(f32)
    n = parts.shape[0]
    means, stats = parts[:, :32, :], parts[:, 32:40, :]
    stats = jnp.concatenate([stats] * 4, axis=1).reshape(n * 32, WIDTH)
    at = iota((n * 32, WIDTH), 1) - iota((n * 32, WIDTH), 0) % 32
    ones = jnp.ones((WIDTH, WIDTH), bf16)
    peaks = dot(jnp.where(at == 0, stats, 0.0).astype(bf16), ones).reshape(n, 32, WIDTH)
    totals = dot(jnp.where((at == 32) | (at == 64), stats, 0.0).astype(bf16), ones)
    totals = totals.reshape(n, 32, WIDTH)
    peak = jnp.max(peaks, axis=0)
    factors = jnp.exp(peaks - peak[None]) * totals
    total = jnp.sum(factors, axis=0)
    mean = jnp.sum(factors * means, axis=0) / jnp.where(total > 0.0, total, 1.0)
    return peak, total, mean


def join(got, out):
    peak, total, mean = merged(got)
    hi, rest = split(total)
    at = iota((32, WIDTH), 1) - iota((32, WIDTH), 0)
    stat = jnp.where(at == 0, peak, jnp.where(at == 32, hi, jnp.where(at == 64, rest, 0.0)))
    stat = jnp.broadcast_to(jnp.sum(stat, axis=0, keepdims=True), (8, WIDTH))
    block = jnp.concatenate([mean, stat], axis=0).astype(bf16)
    out[...] = jnp.broadcast_to(block[None], out.shape)


def finish(got, out):
    peak, total, mean = merged(got)
    to, of = iota((32, 32), 0), iota((32, 32), 1)
    move = (to // 16 == (of // 4) % 2) & ((to // 4) % 4 == of % 4) & (to % 4 == of // 8)
    moved = dot(jnp.where(move, 1.0, 0.0).astype(bf16), mean.astype(bf16)).astype(bf16)
    out[...] = jnp.broadcast_to(moved[None], out.shape)


def project(attended, weight, out):
    features = jnp.concatenate(
        [attended[i, COUNT * j : COUNT * (j + 1), :] for i in range(SIDE) for j in range(2)],
        axis=1,
    )
    out[...] = jnp.broadcast_to(dot(features, weight[...])[None], out.shape)


def normalise(parts, stream_in, gain, out, stream_out):
    stream = stream_in[...] + jnp.sum(parts[...], axis=0)
    for i in range(STEPS):
        stream_out[i] = stream[ROWS * i : ROWS * (i + 1)]
    squares = jnp.sum(stream * stream, axis=1, keepdims=True)
    hi, rest = split(squares)
    mid, rest = split(rest)
    at = iota((COUNT, WIDTH), 1) - iota((COUNT, WIDTH), 0)
    stat = jnp.where(at == 0, hi, jnp.where(at == 32, mid, jnp.where(at == 64, rest, 0.0)))
    stat = jnp.broadcast_to(jnp.sum(stat, axis=0, keepdims=True), (8, WIDTH))
    scaled = stream * gain[...]
    block = jnp.concatenate([scaled[:, :WIDTH], scaled[:, WIDTH:], stat], axis=0).astype(bf16)
    out[...] = jnp.broadcast_to(block[None], out.shape)


def feed(got, weight, out):
    n = got.shape[0]
    tokens = jnp.concatenate(
        [got[s, COUNT * j : COUNT * (j + 1), :] for s in range(n) for j in range(2)], axis=1
    )
    stats = jnp.sum(got[:, 32:40, :].astype(f32), axis=0)
    stats = jnp.concatenate([stats, stats], axis=0)
    at = iota((COUNT, WIDTH), 1) - iota((COUNT, WIDTH), 0)
    stats = jnp.where((at == 0) | (at == 32) | (at == 64), stats, 0.0)
    squares = jnp.sum(stats, axis=1, keepdims=True)
    inverse = lax.rsqrt(squares / (n * 2 * WIDTH) + epsilon)
    gate = dot_t(tokens, weight[0]) * inverse
    up = dot_t(tokens, weight[1]) * inverse
    hidden = gate / (1.0 + jnp.exp(-gate)) * up
    for i in range(STEPS):
        out[i] = hidden[ROWS * i : ROWS * (i + 1)].astype(bf16)


def send(x, axis):
    return lax.all_to_all(x, axis, split_axis=0, concat_axis=0, tiled=True)


def shards(
    queries,
    drafted_key_value,
    paged_key_value,
    block_table,
    page_count,
    tail_fill,
    out_weight,
    stream_in,
    norm_gain,
    gate_up,
):
    seq_index = lax.axis_index(("z", "y"))
    seq_count = lax.axis_size(("z", "y"))
    pages, page_len = paged_key_value.shape[2], paged_key_value.shape[3]
    columns = out_weight.shape[1]
    units = gate_up.shape[1]

    shape = jax.ShapeDtypeStruct
    mine = call(copies, shape((seq_count, STEPS, ROWS * QUARTER), bf16))(queries)
    gathered = send(mine, ("z", "y"))
    held = (paged_key_value, out_weight)
    paged_key_value, out_weight = pl.pallas_call(
        fetch,
        in_specs=[pl.BlockSpec(memory_space=pl.ANY)] * len(held),
        out_specs=[pl.BlockSpec(memory_space=pltpu.VMEM)] * len(held),
        out_shape=[shape(x.shape, x.dtype) for x in held],
        scratch_shapes=[pltpu.SemaphoreType.DMA((len(held),))],
    )(*held)

    slots = seq_index * pages + jnp.arange(pages, dtype=jnp.int32)
    page_index = jnp.arange(block_table.shape[1], dtype=jnp.int32)
    held = (block_table[:, :, None] == slots[None, None, :]) & (
        page_index[None, :, None] < page_count[:, None, None]
    )
    last = page_index[None, :] == page_count[:, None] - 1
    fill = jnp.where(last, tail_fill[:, None], page_len)
    filled = jnp.max(jnp.where(held, fill[:, :, None], 0), axis=1)
    bias = jnp.where(jnp.arange(page_len)[None, None, :] < filled[:, :, None], 0.0, low)
    bias = bias.reshape(ROWS, pages * page_len).astype(f32)
    row = jnp.arange(ROWS)[:, None, None]
    step = (jnp.arange(GROUP * STEPS) % STEPS)[None, :, None]
    key = jnp.arange(COUNT)[None, None, :]
    ok = (key % ROWS == row) & (key // ROWS <= step) & (row == seq_index)
    fresh_bias = jnp.where(ok, 0.0, low).astype(f32)
    fresh_keys = drafted_key_value[:, :, 0, 0].reshape(COUNT, WIDTH)
    fresh_values = drafted_key_value[:, :, 1, 0].reshape(COUNT, WIDTH)

    block = call(
        attend, shape((SIDE, 40, WIDTH), bf16), [pltpu.VMEM((SIDE, 40, WIDTH), f32)]
    )(gathered, paged_key_value, fresh_keys, fresh_values, bias, fresh_bias)
    block = call(join, shape((SIDE, 40, WIDTH), bf16))(send(block, "y"))
    attended = call(finish, shape((SIDE, 32, WIDTH), bf16))(send(block, "z"))
    partial_sum = call(project, shape((SIDE, COUNT, columns), f32))(
        send(attended, "y"), out_weight
    )
    scaled, stream = call(
        normalise,
        (shape((seq_count, 40, WIDTH), bf16), shape((STEPS, ROWS, columns), f32)),
    )(
        send(partial_sum, ("x", "core")),
        stream_in.reshape(COUNT, columns),
        norm_gain.reshape(1, columns),
    )
    hidden = call(feed, shape((STEPS, ROWS, units), bf16))(send(scaled, ("z", "y")), gate_up)
    return hidden, stream


def solution(mesh):
    fine = Mesh(mesh.devices.reshape(4, 2, 8, 8), ("x", "core", "z", "y"))
    kvh, seq = ("x", "core"), ("z", "y")
    placed = (
        P(None, None, kvh + seq),
        P(None, None, None, kvh, None),
        P(None, kvh, seq, None, None),
        P(),
        P(),
        P(),
        P(kvh, seq),
        P(None, None, seq),
        P(seq),
        P(None, kvh + seq, None),
    )
    return jax.shard_map(
        shards,
        mesh=fine,
        in_specs=placed,
        out_specs=(P(None, None, kvh + seq), P(None, None, seq)),
        check_vma=False,
    )
```

```python
import jax
import jax.numpy as jnp
from jax import lax
from jax.experimental import pallas as pl
from jax.experimental.pallas import tpu as pltpu
from jax.sharding import Mesh
from jax.sharding import PartitionSpec as P

QUERY_HEADS = 128
KEY_VALUE_HEADS = 8
GROUP = QUERY_HEADS // KEY_VALUE_HEADS
WIDTH = 128
STEPS = 4
ROWS = 4
COUNT = STEPS * ROWS
QUARTER = 32
SIDE = 8

low = -1e30
floor = -1e29
epsilon = 1e-05
f32 = jnp.float32
bf16 = jnp.bfloat16


def iota(shape, axis):
    return lax.broadcasted_iota(jnp.int32, shape, axis)


def dot(a, b):
    return lax.dot_general(a, b, (((1,), (0,)), ((), ())), preferred_element_type=f32)


def dot_t(a, b):
    return lax.dot_general(a, b, (((1,), (1,)), ((), ())), preferred_element_type=f32)


def split(x):
    hi = x.astype(bf16).astype(f32)
    return hi, x - hi


def call(body, out_shape, inputs="", scratch=(), limit=32 * 2**20):
    spaces = {"v": pltpu.VMEM, "h": pl.ANY, "s": pltpu.SMEM}
    return pl.pallas_call(
        body,
        out_shape=out_shape,
        in_specs=[pl.BlockSpec(memory_space=spaces[c]) for c in inputs],
        scratch_shapes=list(scratch),
        compiler_params=pltpu.CompilerParams(vmem_limit_bytes=limit),
    )


def begin(pairs, sems):
    moves = [pltpu.make_async_copy(a, b, sems.at[i]) for i, (a, b) in enumerate(pairs)]
    for move in moves:
        move.start()
    return moves


def copies(queries, out):
    x = queries[...].astype(f32)
    x = jnp.concatenate([x[:, r, :] for r in range(ROWS)], axis=1).astype(bf16)
    out[...] = jnp.broadcast_to(x[None], out.shape)


def prepare(
    table, count, tail, index, drafted, paged, bias, fresh_bias, fresh_keys, fresh_values, held, sems
):
    moves = begin([(paged, held)], sems)
    pages, page_len = paged.shape[2], paged.shape[3]
    row, page = iota(table.shape, 0), iota(table.shape, 1)
    counts = tails = jnp.zeros(table.shape, jnp.int32)
    for r in range(ROWS):
        counts = jnp.where(row == r, count[r], counts)
        tails = jnp.where(row == r, tail[r], tails)
    fill = jnp.where(page == counts - 1, tails, page_len).astype(f32)
    fill = jnp.where(page < counts, fill, 0.0)
    slots = table[...]
    token = iota((ROWS, page_len), 1).astype(f32)
    for p in range(pages):
        filled = jnp.where(slots == index[0] * pages + p, fill, 0.0)
        filled = jnp.max(filled, axis=1, keepdims=True)
        bias[:, p * page_len : (p + 1) * page_len] = jnp.where(token < filled, 0.0, low)
    step = iota((GROUP * STEPS, COUNT), 0) % STEPS
    key = iota((GROUP * STEPS, COUNT), 1)
    causal = key // ROWS <= step
    for r in range(ROWS):
        ok = causal & (key % ROWS == r) & (index[0] == r)
        fresh_bias[r] = jnp.where(ok, 0.0, low)
    both = drafted[...].astype(f32)
    fresh_keys[...] = both[:, 0, :].astype(bf16)
    fresh_values[...] = both[:, 1, :].astype(bf16)
    moves[0].wait()


def attend(
    gathered,
    paged,
    fresh_keys,
    fresh_values,
    bias,
    fresh_bias,
    out_weight,
    gate_up,
    out,
    out_weight_held,
    gate_up_held,
    block,
    sems,
):
    moves = begin([(out_weight, out_weight_held), (gate_up, gate_up_held)], sems)
    sent = jnp.concatenate([gathered[:, i, :].astype(f32) for i in range(STEPS)], axis=0)
    shape = (STEPS * GROUP * 4, WIDTH)
    quarter = iota(shape, 0) % 4
    diagonal = iota(shape, 1) // QUARTER == quarter
    turned = [sent] + [pltpu.roll(sent, QUARTER * d, 1) for d in range(1, 4)]
    pick_row = iota((GROUP * STEPS, shape[0]), 0)
    pick_col = iota((GROUP * STEPS, shape[0]), 1)
    pick = (pick_row // STEPS == (pick_col // 4) % GROUP) & (
        pick_row % STEPS == pick_col // (4 * GROUP)
    )
    pick = jnp.where(pick, 1.0, 0.0).astype(bf16)
    keys = paged[0, 0].reshape(-1, WIDTH)
    values = paged[1, 0].reshape(-1, WIDTH)
    fresh_k = fresh_keys[...]
    fresh_v = fresh_values[...]
    ones = jnp.ones((keys.shape[0], WIDTH), bf16)
    fresh_ones = jnp.ones((fresh_k.shape[0], WIDTH), bf16)
    scale = WIDTH ** (-0.5)
    lane = iota((GROUP * STEPS, WIDTH), 1)
    place = iota((GROUP * STEPS, WIDTH), 0) % 8
    stats = None
    for r in range(ROWS):
        chosen = turned[(3 - r) % 4]
        for c in range(3):
            chosen = jnp.where(quarter == c, turned[(c - r) % 4], chosen)
        chosen = jnp.where(diagonal, chosen, 0.0).astype(bf16)
        query = dot(pick, chosen).astype(bf16)
        scores = dot_t(query, keys) * scale + bias[r : r + 1, :]
        fresh = dot_t(query, fresh_k) * scale + fresh_bias[r]
        peak = jnp.maximum(
            jnp.max(scores, axis=1, keepdims=True), jnp.max(fresh, axis=1, keepdims=True)
        )
        peak = jnp.maximum(peak, floor).astype(bf16).astype(f32)
        weights = jnp.exp(scores - peak).astype(bf16)
        fresh_weights = jnp.exp(fresh - peak).astype(bf16)
        total = dot(weights, ones) + dot(fresh_weights, fresh_ones)
        summed = dot(weights, values) + dot(fresh_weights, fresh_v)
        mean = summed / jnp.where(total > 0.0, total, 1.0)
        block[:, 8 * r : 8 * r + 8, :] = mean.reshape(SIDE, 8, WIDTH)
        hi, rest = split(total)
        at = lane - place - 8 * r
        stat = jnp.where(at == 0, peak, jnp.where(at == 32, hi, jnp.where(at == 64, rest, 0.0)))
        stats = stat if stats is None else stats + stat
    stats = stats.reshape(SIDE, 8, WIDTH)
    block[:, 32:40, :] = jnp.broadcast_to(
        jnp.sum(stats, axis=1, keepdims=True), (SIDE, 8, WIDTH)
    )
    out[...] = block[...].astype(bf16)
    for move in moves:
        move.wait()


def merged(got):
    parts = got[...].astype(f32)
    n = parts.shape[0]
    means, stats = parts[:, :32, :], parts[:, 32:40, :]
    stats = jnp.concatenate([stats] * 4, axis=1).reshape(n * 32, WIDTH)
    at = iota((n * 32, WIDTH), 1) - iota((n * 32, WIDTH), 0) % 32
    ones = jnp.ones((WIDTH, WIDTH), bf16)
    peaks = dot(jnp.where(at == 0, stats, 0.0).astype(bf16), ones).reshape(n, 32, WIDTH)
    totals = dot(jnp.where((at == 32) | (at == 64), stats, 0.0).astype(bf16), ones)
    totals = totals.reshape(n, 32, WIDTH)
    peak = jnp.max(peaks, axis=0)
    factors = jnp.exp(peaks - peak[None]) * totals
    total = jnp.sum(factors, axis=0)
    mean = jnp.sum(factors * means, axis=0) / jnp.where(total > 0.0, total, 1.0)
    return peak, total, mean


def join(got, out):
    peak, total, mean = merged(got)
    hi, rest = split(total)
    at = iota((32, WIDTH), 1) - iota((32, WIDTH), 0)
    stat = jnp.where(at == 0, peak, jnp.where(at == 32, hi, jnp.where(at == 64, rest, 0.0)))
    stat = jnp.broadcast_to(jnp.sum(stat, axis=0, keepdims=True), (8, WIDTH))
    block = jnp.concatenate([mean, stat], axis=0).astype(bf16)
    out[...] = jnp.broadcast_to(block[None], out.shape)


def finish(got, out):
    peak, total, mean = merged(got)
    to, of = iota((32, 32), 0), iota((32, 32), 1)
    move = (to // 16 == (of // 4) % 2) & ((to // 4) % 4 == of % 4) & (to % 4 == of // 8)
    moved = dot(jnp.where(move, 1.0, 0.0).astype(bf16), mean.astype(bf16)).astype(bf16)
    out[...] = jnp.broadcast_to(moved[None], out.shape)


def project(attended, weight, out):
    features = jnp.concatenate(
        [attended[i, COUNT * j : COUNT * (j + 1), :] for i in range(SIDE) for j in range(2)],
        axis=1,
    )
    out[...] = jnp.broadcast_to(dot(features, weight[...]).astype(bf16)[None], out.shape)


def normalise(parts, stream_in, gain, out, stream_out, rows):
    for i in range(STEPS):
        rows[ROWS * i : ROWS * (i + 1), :] = stream_in[i]
    stream = rows[...] + jnp.sum(parts[...].astype(f32), axis=0)
    for i in range(STEPS):
        stream_out[i] = stream[ROWS * i : ROWS * (i + 1)]
    squares = jnp.sum(stream * stream, axis=1, keepdims=True)
    hi, rest = split(squares)
    mid, rest = split(rest)
    at = iota((COUNT, WIDTH), 1) - iota((COUNT, WIDTH), 0)
    stat = jnp.where(at == 0, hi, jnp.where(at == 32, mid, jnp.where(at == 64, rest, 0.0)))
    stat = jnp.broadcast_to(jnp.sum(stat, axis=0, keepdims=True), (8, WIDTH))
    scaled = stream * gain[...]
    block = jnp.concatenate([scaled[:, :WIDTH], scaled[:, WIDTH:], stat], axis=0).astype(bf16)
    out[...] = jnp.broadcast_to(block[None], out.shape)


def feed(got, weight, out):
    n = got.shape[0]
    tokens = jnp.concatenate(
        [got[s, COUNT * j : COUNT * (j + 1), :] for s in range(n) for j in range(2)], axis=1
    )
    stats = jnp.sum(got[:, 32:40, :].astype(f32), axis=0)
    stats = jnp.concatenate([stats, stats], axis=0)
    at = iota((COUNT, WIDTH), 1) - iota((COUNT, WIDTH), 0)
    stats = jnp.where((at == 0) | (at == 32) | (at == 64), stats, 0.0)
    squares = jnp.sum(stats, axis=1, keepdims=True)
    inverse = lax.rsqrt(squares / (n * 2 * WIDTH) + epsilon)
    gate = dot_t(tokens, weight[0]) * inverse
    up = dot_t(tokens, weight[1]) * inverse
    hidden = gate / (1.0 + jnp.exp(-gate)) * up
    for i in range(STEPS):
        out[i] = hidden[ROWS * i : ROWS * (i + 1)].astype(bf16)


def send(x, axis):
    return lax.all_to_all(x, axis, split_axis=0, concat_axis=0, tiled=True)


def shards(
    queries,
    drafted_key_value,
    paged_key_value,
    block_table,
    page_count,
    tail_fill,
    out_weight,
    stream_in,
    norm_gain,
    gate_up,
):
    seq_index = lax.axis_index(("z", "y"))
    seq_count = lax.axis_size(("z", "y"))
    pages, page_len = paged_key_value.shape[2], paged_key_value.shape[3]
    columns = out_weight.shape[1]
    units = gate_up.shape[1]

    shape = jax.ShapeDtypeStruct
    dma = pltpu.SemaphoreType.DMA
    mine = call(copies, shape((seq_count, STEPS, ROWS * QUARTER), bf16), "v")(queries)
    gathered = send(mine, ("z", "y"))

    drafted = drafted_key_value.transpose(0, 1, 3, 2, 4).reshape(COUNT, 2, WIDTH)
    bias, fresh_bias, fresh_keys, fresh_values, held = call(
        prepare,
        (
            shape((ROWS, pages * page_len), f32),
            shape((ROWS, GROUP * STEPS, COUNT), f32),
            shape((COUNT, WIDTH), bf16),
            shape((COUNT, WIDTH), bf16),
            shape(paged_key_value.shape, bf16),
        ),
        "vsssvh",
        [dma((1,))],
        limit=8 * 2**20,
    )(block_table, page_count, tail_fill, seq_index.reshape(1), drafted, paged_key_value)
    block, weight, gates = call(
        attend,
        (
            shape((SIDE, 40, WIDTH), bf16),
            shape(out_weight.shape, bf16),
            shape(gate_up.shape, bf16),
        ),
        "vvvvvvhh",
        [pltpu.VMEM((SIDE, 40, WIDTH), f32), dma((2,))],
    )(gathered, held, fresh_keys, fresh_values, bias, fresh_bias, out_weight, gate_up)
    block = call(join, shape((SIDE, 40, WIDTH), bf16), "v")(send(block, "y"))
    attended = call(finish, shape((SIDE, 32, WIDTH), bf16), "v")(send(block, "z"))
    partial_sum = call(project, shape((SIDE, COUNT, columns), bf16), "vv")(
        send(attended, "y"), weight
    )
    scaled, stream = call(
        normalise,
        (shape((seq_count, 40, WIDTH), bf16), shape((STEPS, ROWS, columns), f32)),
        "vvv",
        [pltpu.VMEM((COUNT, columns), f32)],
    )(send(partial_sum, ("x", "core")), stream_in, norm_gain.reshape(1, columns))
    hidden = call(feed, shape((STEPS, ROWS, units), bf16), "vv")(
        send(scaled, ("z", "y")), gates
    )
    return hidden, stream


def solution(mesh):
    fine = Mesh(mesh.devices.reshape(4, 2, 8, 8), ("x", "core", "z", "y"))
    kvh, seq = ("x", "core"), ("z", "y")
    placed = (
        P(None, None, kvh + seq),
        P(None, None, None, kvh, None),
        P(None, kvh, seq, None, None),
        P(),
        P(),
        P(),
        P(kvh, seq),
        P(None, None, seq),
        P(seq),
        P(None, kvh + seq, None),
    )
    return jax.shard_map(
        shards,
        mesh=fine,
        in_specs=placed,
        out_specs=(P(None, None, kvh + seq), P(None, None, seq)),
        check_vma=False,
    )
```

```python
import jax
import jax.numpy as jnp
from jax import lax
from jax.experimental import pallas as pl
from jax.experimental.pallas import tpu as pltpu
from jax.sharding import Mesh
from jax.sharding import PartitionSpec as P

QUERY_HEADS = 128
KEY_VALUE_HEADS = 8
GROUP = QUERY_HEADS // KEY_VALUE_HEADS
WIDTH = 128
STEPS = 4
ROWS = 4
COUNT = STEPS * ROWS
QUARTER = 32
SIDE = 8

low = -1e30
floor = -1e29
epsilon = 1e-05
f32 = jnp.float32
bf16 = jnp.bfloat16


def iota(shape, axis):
    return lax.broadcasted_iota(jnp.int32, shape, axis)


def dot(a, b):
    return lax.dot_general(a, b, (((1,), (0,)), ((), ())), preferred_element_type=f32)


def dot_t(a, b):
    return lax.dot_general(a, b, (((1,), (1,)), ((), ())), preferred_element_type=f32)


def split(x):
    hi = x.astype(bf16).astype(f32)
    return hi, x - hi


def call(body, out_shape, inputs="", scratch=(), limit=32 * 2**20, moved=2**24):
    spaces = {"v": pltpu.VMEM, "h": pl.ANY, "s": pltpu.SMEM}
    return pl.pallas_call(
        body,
        out_shape=out_shape,
        in_specs=[pl.BlockSpec(memory_space=spaces[c]) for c in inputs],
        scratch_shapes=list(scratch),
        cost_estimate=pl.CostEstimate(flops=2**26, bytes_accessed=moved, transcendentals=2**18),
        compiler_params=pltpu.CompilerParams(vmem_limit_bytes=limit),
    )


def begin(pairs, sems):
    moves = [pltpu.make_async_copy(a, b, sems.at[i]) for i, (a, b) in enumerate(pairs)]
    for move in moves:
        move.start()
    return moves


def copies(queries, out):
    x = queries[...].astype(f32)
    x = jnp.concatenate([x[:, r, :] for r in range(ROWS)], axis=1).astype(bf16)
    out[...] = jnp.broadcast_to(x[None], out.shape)


def tie(table, weight, out):
    out[...] = table[...]


def prepare(
    table, count, tail, index, drafted, paged, bias, fresh_bias, fresh_keys, fresh_values, held, sems
):
    moves = begin([(paged, held)], sems)
    pages, page_len = paged.shape[2], paged.shape[3]
    row, page = iota(table.shape, 0), iota(table.shape, 1)
    counts = tails = jnp.zeros(table.shape, jnp.int32)
    for r in range(ROWS):
        counts = jnp.where(row == r, count[r], counts)
        tails = jnp.where(row == r, tail[r], tails)
    fill = jnp.where(page == counts - 1, tails, page_len).astype(f32)
    fill = jnp.where(page < counts, fill, 0.0)
    slots = table[...]
    token = iota((ROWS, page_len), 1).astype(f32)
    for p in range(pages):
        filled = jnp.where(slots == index[0] * pages + p, fill, 0.0)
        filled = jnp.max(filled, axis=1, keepdims=True)
        bias[:, p * page_len : (p + 1) * page_len] = jnp.where(token < filled, 0.0, low)
    step = iota((GROUP * STEPS, COUNT), 0) % STEPS
    key = iota((GROUP * STEPS, COUNT), 1)
    causal = key // ROWS <= step
    for r in range(ROWS):
        ok = causal & (key % ROWS == r) & (index[0] == r)
        fresh_bias[r] = jnp.where(ok, 0.0, low)
    both = drafted[...].astype(f32)
    fresh_keys[...] = both[:, 0, :].astype(bf16)
    fresh_values[...] = both[:, 1, :].astype(bf16)
    moves[0].wait()


def attend(
    gathered,
    paged,
    fresh_keys,
    fresh_values,
    bias,
    fresh_bias,
    out,
    block,
):
    sent = jnp.concatenate([gathered[:, i, :].astype(f32) for i in range(STEPS)], axis=0)
    shape = (STEPS * GROUP * 4, WIDTH)
    quarter = iota(shape, 0) % 4
    diagonal = iota(shape, 1) // QUARTER == quarter
    turned = [sent] + [pltpu.roll(sent, QUARTER * d, 1) for d in range(1, 4)]
    pick_row = iota((GROUP * STEPS, shape[0]), 0)
    pick_col = iota((GROUP * STEPS, shape[0]), 1)
    pick = (pick_row // STEPS == (pick_col // 4) % GROUP) & (
        pick_row % STEPS == pick_col // (4 * GROUP)
    )
    pick = jnp.where(pick, 1.0, 0.0).astype(bf16)
    keys = paged[0, 0].reshape(-1, WIDTH)
    values = paged[1, 0].reshape(-1, WIDTH)
    fresh_k = fresh_keys[...]
    fresh_v = fresh_values[...]
    ones = jnp.ones((keys.shape[0], WIDTH), bf16)
    fresh_ones = jnp.ones((fresh_k.shape[0], WIDTH), bf16)
    scale = WIDTH ** (-0.5)
    lane = iota((GROUP * STEPS, WIDTH), 1)
    place = iota((GROUP * STEPS, WIDTH), 0) % 8
    stats = None
    for r in range(ROWS):
        chosen = turned[(3 - r) % 4]
        for c in range(3):
            chosen = jnp.where(quarter == c, turned[(c - r) % 4], chosen)
        chosen = jnp.where(diagonal, chosen, 0.0).astype(bf16)
        query = dot(pick, chosen).astype(bf16)
        scores = dot_t(query, keys) * scale + bias[r : r + 1, :]
        fresh = dot_t(query, fresh_k) * scale + fresh_bias[r]
        peak = jnp.maximum(
            jnp.max(scores, axis=1, keepdims=True), jnp.max(fresh, axis=1, keepdims=True)
        )
        peak = jnp.maximum(peak, floor).astype(bf16).astype(f32)
        weights = jnp.exp(scores - peak).astype(bf16)
        fresh_weights = jnp.exp(fresh - peak).astype(bf16)
        total = dot(weights, ones) + dot(fresh_weights, fresh_ones)
        summed = dot(weights, values) + dot(fresh_weights, fresh_v)
        mean = summed / jnp.where(total > 0.0, total, 1.0)
        block[:, 8 * r : 8 * r + 8, :] = mean.reshape(SIDE, 8, WIDTH)
        hi, rest = split(total)
        at = lane - place - 8 * r
        stat = jnp.where(at == 0, peak, jnp.where(at == 32, hi, jnp.where(at == 64, rest, 0.0)))
        stats = stat if stats is None else stats + stat
    stats = stats.reshape(SIDE, 8, WIDTH)
    block[:, 32:40, :] = jnp.broadcast_to(
        jnp.sum(stats, axis=1, keepdims=True), (SIDE, 8, WIDTH)
    )
    out[...] = block[...].astype(bf16)


def merged(got):
    parts = got[...].astype(f32)
    n = parts.shape[0]
    means, stats = parts[:, :32, :], parts[:, 32:40, :]
    stats = jnp.concatenate([stats] * 4, axis=1).reshape(n * 32, WIDTH)
    at = iota((n * 32, WIDTH), 1) - iota((n * 32, WIDTH), 0) % 32
    ones = jnp.ones((WIDTH, WIDTH), bf16)
    peaks = dot(jnp.where(at == 0, stats, 0.0).astype(bf16), ones).reshape(n, 32, WIDTH)
    totals = dot(jnp.where((at == 32) | (at == 64), stats, 0.0).astype(bf16), ones)
    totals = totals.reshape(n, 32, WIDTH)
    peak = jnp.max(peaks, axis=0)
    factors = jnp.exp(peaks - peak[None]) * totals
    total = jnp.sum(factors, axis=0)
    mean = jnp.sum(factors * means, axis=0) / jnp.where(total > 0.0, total, 1.0)
    return peak, total, mean


def join(got, out):
    peak, total, mean = merged(got)
    hi, rest = split(total)
    at = iota((32, WIDTH), 1) - iota((32, WIDTH), 0)
    stat = jnp.where(at == 0, peak, jnp.where(at == 32, hi, jnp.where(at == 64, rest, 0.0)))
    stat = jnp.broadcast_to(jnp.sum(stat, axis=0, keepdims=True), (8, WIDTH))
    block = jnp.concatenate([mean, stat], axis=0).astype(bf16)
    out[...] = jnp.broadcast_to(block[None], out.shape)


def finish(got, out):
    peak, total, mean = merged(got)
    to, of = iota((32, 32), 0), iota((32, 32), 1)
    move = (to // 16 == (of // 4) % 2) & ((to // 4) % 4 == of % 4) & (to % 4 == of // 8)
    moved = dot(jnp.where(move, 1.0, 0.0).astype(bf16), mean.astype(bf16)).astype(bf16)
    out[...] = jnp.broadcast_to(moved[None], out.shape)


def project(attended, weight, out):
    features = jnp.concatenate(
        [attended[i, COUNT * j : COUNT * (j + 1), :] for i in range(SIDE) for j in range(2)],
        axis=1,
    )
    out[...] = jnp.broadcast_to(dot(features, weight[...]).astype(bf16)[None], out.shape)


def normalise(parts, stream_in, gain, out, stream_out, rows):
    for i in range(STEPS):
        rows[ROWS * i : ROWS * (i + 1), :] = stream_in[i]
    stream = rows[...] + jnp.sum(parts[...].astype(f32), axis=0)
    for i in range(STEPS):
        stream_out[i] = stream[ROWS * i : ROWS * (i + 1)]
    squares = jnp.sum(stream * stream, axis=1, keepdims=True)
    hi, rest = split(squares)
    mid, rest = split(rest)
    at = iota((COUNT, WIDTH), 1) - iota((COUNT, WIDTH), 0)
    stat = jnp.where(at == 0, hi, jnp.where(at == 32, mid, jnp.where(at == 64, rest, 0.0)))
    stat = jnp.broadcast_to(jnp.sum(stat, axis=0, keepdims=True), (8, WIDTH))
    scaled = stream * gain[...]
    block = jnp.concatenate([scaled[:, :WIDTH], scaled[:, WIDTH:], stat], axis=0).astype(bf16)
    out[...] = jnp.broadcast_to(block[None], out.shape)


def feed(got, weight, out):
    n = got.shape[0]
    tokens = jnp.concatenate(
        [got[s, COUNT * j : COUNT * (j + 1), :] for s in range(n) for j in range(2)], axis=1
    )
    stats = jnp.sum(got[:, 32:40, :].astype(f32), axis=0)
    stats = jnp.concatenate([stats, stats], axis=0)
    at = iota((COUNT, WIDTH), 1) - iota((COUNT, WIDTH), 0)
    stats = jnp.where((at == 0) | (at == 32) | (at == 64), stats, 0.0)
    squares = jnp.sum(stats, axis=1, keepdims=True)
    inverse = lax.rsqrt(squares / (n * 2 * WIDTH) + epsilon)
    gate = dot_t(tokens, weight[0]) * inverse
    up = dot_t(tokens, weight[1]) * inverse
    hidden = gate / (1.0 + jnp.exp(-gate)) * up
    for i in range(STEPS):
        out[i] = hidden[ROWS * i : ROWS * (i + 1)].astype(bf16)


def send(x, axis):
    return lax.all_to_all(x, axis, split_axis=0, concat_axis=0, tiled=True)


def shards(
    queries,
    drafted_key_value,
    paged_key_value,
    block_table,
    page_count,
    tail_fill,
    out_weight,
    stream_in,
    norm_gain,
    gate_up,
):
    seq_index = lax.axis_index(("z", "y"))
    seq_count = lax.axis_size(("z", "y"))
    pages, page_len = paged_key_value.shape[2], paged_key_value.shape[3]
    columns = out_weight.shape[1]
    units = gate_up.shape[1]

    shape = jax.ShapeDtypeStruct
    dma = pltpu.SemaphoreType.DMA
    mine = call(copies, shape((seq_count, STEPS, ROWS * QUARTER), bf16), "v")(queries)
    gathered = send(mine, ("z", "y"))

    drafted = drafted_key_value.transpose(0, 1, 3, 2, 4).reshape(COUNT, 2, WIDTH)
    table = call(tie, shape(block_table.shape, jnp.int32), "vh", limit=62 * 2**20)(
        block_table, gate_up
    )
    bias, fresh_bias, fresh_keys, fresh_values, held = call(
        prepare,
        (
            shape((ROWS, pages * page_len), f32),
            shape((ROWS, GROUP * STEPS, COUNT), f32),
            shape((COUNT, WIDTH), bf16),
            shape((COUNT, WIDTH), bf16),
            shape(paged_key_value.shape, bf16),
        ),
        "vsssvh",
        [dma((1,))],
        limit=8 * 2**20,
    )(table, page_count, tail_fill, seq_index.reshape(1), drafted, paged_key_value)
    block = call(
        attend,
        shape((SIDE, 40, WIDTH), bf16),
        "vvvvvv",
        [pltpu.VMEM((SIDE, 40, WIDTH), f32)],
    )(gathered, held, fresh_keys, fresh_values, bias, fresh_bias)
    block = call(join, shape((SIDE, 40, WIDTH), bf16), "v")(send(block, "y"))
    attended = call(finish, shape((SIDE, 32, WIDTH), bf16), "v")(send(block, "z"))
    partial_sum = call(project, shape((SIDE, COUNT, columns), bf16), "vv")(
        send(attended, "y"), out_weight
    )
    scaled, stream = call(
        normalise,
        (shape((seq_count, 40, WIDTH), bf16), shape((STEPS, ROWS, columns), f32)),
        "vvv",
        [pltpu.VMEM((COUNT, columns), f32)],
    )(send(partial_sum, ("x", "core")), stream_in, norm_gain.reshape(1, columns))
    hidden = call(feed, shape((STEPS, ROWS, units), bf16), "vv")(
        send(scaled, ("z", "y")), gate_up
    )
    return hidden, stream


def solution(mesh):
    fine = Mesh(mesh.devices.reshape(4, 2, 8, 8), ("x", "core", "z", "y"))
    kvh, seq = ("x", "core"), ("z", "y")
    placed = (
        P(None, None, kvh + seq),
        P(None, None, None, kvh, None),
        P(None, kvh, seq, None, None),
        P(),
        P(),
        P(),
        P(kvh, seq),
        P(None, None, seq),
        P(seq),
        P(None, kvh + seq, None),
    )
    return jax.shard_map(
        shards,
        mesh=fine,
        in_specs=placed,
        out_specs=(P(None, None, kvh + seq), P(None, None, seq)),
        check_vma=False,
    )
```

```python
import jax
import jax.numpy as jnp
from jax import lax
from jax.experimental import pallas as pl
from jax.experimental.pallas import tpu as pltpu
from jax.sharding import Mesh
from jax.sharding import PartitionSpec as P

QUERY_HEADS = 128
KEY_VALUE_HEADS = 8
GROUP = QUERY_HEADS // KEY_VALUE_HEADS
WIDTH = 128
STEPS = 4
ROWS = 4
COUNT = STEPS * ROWS
QUARTER = 32
SIDE = 8

low = -1e30
floor = -1e29
epsilon = 1e-05
f32 = jnp.float32
bf16 = jnp.bfloat16


def iota(shape, axis):
    return lax.broadcasted_iota(jnp.int32, shape, axis)


def dot(a, b):
    return lax.dot_general(a, b, (((1,), (0,)), ((), ())), preferred_element_type=f32)


def dot_t(a, b):
    return lax.dot_general(a, b, (((1,), (1,)), ((), ())), preferred_element_type=f32)


def split(x):
    hi = x.astype(bf16).astype(f32)
    return hi, x - hi


def call(body, out_shape, inputs="", scratch=(), limit=32 * 2**20, moved=2**24):
    spaces = {"v": pltpu.VMEM, "h": pl.ANY, "s": pltpu.SMEM}
    return pl.pallas_call(
        body,
        out_shape=out_shape,
        in_specs=[pl.BlockSpec(memory_space=spaces[c]) for c in inputs],
        scratch_shapes=list(scratch),
        cost_estimate=pl.CostEstimate(flops=2**26, bytes_accessed=moved, transcendentals=2**18),
        compiler_params=pltpu.CompilerParams(vmem_limit_bytes=limit),
    )


def begin(pairs, sems):
    moves = [pltpu.make_async_copy(a, b, sems.at[i]) for i, (a, b) in enumerate(pairs)]
    for move in moves:
        move.start()
    return moves


def copies(queries, out):
    x = queries[...].astype(f32)
    x = jnp.concatenate([x[:, r, :] for r in range(ROWS)], axis=1).astype(bf16)
    out[...] = jnp.broadcast_to(x[None], out.shape)


def tie(table, weight, out):
    out[...] = table[...]


def prepare(
    table, count, tail, index, drafted, paged, bias, fresh_bias, fresh_keys, fresh_values, held, sems
):
    moves = begin([(paged, held)], sems)
    pages, page_len = paged.shape[2], paged.shape[3]
    row, page = iota(table.shape, 0), iota(table.shape, 1)
    counts = tails = jnp.zeros(table.shape, jnp.int32)
    for r in range(ROWS):
        counts = jnp.where(row == r, count[r], counts)
        tails = jnp.where(row == r, tail[r], tails)
    fill = jnp.where(page == counts - 1, tails, page_len).astype(f32)
    fill = jnp.where(page < counts, fill, 0.0)
    slots = table[...]
    token = iota((ROWS, page_len), 1).astype(f32)
    for p in range(pages):
        filled = jnp.where(slots == index[0] * pages + p, fill, 0.0)
        filled = jnp.max(filled, axis=1, keepdims=True)
        bias[:, p * page_len : (p + 1) * page_len] = jnp.where(token < filled, 0.0, low)
    step = iota((GROUP * STEPS, COUNT), 0) % STEPS
    key = iota((GROUP * STEPS, COUNT), 1)
    causal = key // ROWS <= step
    for r in range(ROWS):
        ok = causal & (key % ROWS == r) & (index[0] == r)
        fresh_bias[r] = jnp.where(ok, 0.0, low)
    both = drafted[...].astype(f32)
    fresh_keys[...] = both[:, 0, :].astype(bf16)
    fresh_values[...] = both[:, 1, :].astype(bf16)
    moves[0].wait()


def attend(
    gathered,
    paged,
    fresh_keys,
    fresh_values,
    bias,
    fresh_bias,
    out,
    block,
):
    sent = jnp.concatenate([gathered[:, i, :].astype(f32) for i in range(STEPS)], axis=0)
    shape = (STEPS * GROUP * 4, WIDTH)
    quarter = iota(shape, 0) % 4
    diagonal = iota(shape, 1) // QUARTER == quarter
    turned = [sent] + [pltpu.roll(sent, QUARTER * d, 1) for d in range(1, 4)]
    pick_row = iota((GROUP * STEPS, shape[0]), 0)
    pick_col = iota((GROUP * STEPS, shape[0]), 1)
    pick = (pick_row // STEPS == (pick_col // 4) % GROUP) & (
        pick_row % STEPS == pick_col // (4 * GROUP)
    )
    pick = jnp.where(pick, 1.0, 0.0).astype(bf16)
    placed = []
    for r in range(ROWS):
        chosen = turned[(3 - r) % 4]
        for c in range(3):
            chosen = jnp.where(quarter == c, turned[(c - r) % 4], chosen)
        placed.append(jnp.where(diagonal, chosen, 0.0).astype(bf16))
    query = dot(pick, jnp.concatenate(placed, axis=1)).astype(bf16)
    query = jnp.concatenate([query[:, r * WIDTH : (r + 1) * WIDTH] for r in range(ROWS)], axis=0)
    keys = paged[0, 0].reshape(-1, WIDTH)
    values = paged[1, 0].reshape(-1, WIDTH)
    values = jnp.concatenate([values, jnp.ones(values.shape, bf16)], axis=1)
    fresh_v = fresh_values[...]
    fresh_v = jnp.concatenate([fresh_v, jnp.ones(fresh_v.shape, bf16)], axis=1)
    each = GROUP * STEPS
    masks = [jnp.broadcast_to(bias[r : r + 1, :], (each, bias.shape[1])) for r in range(ROWS)]
    fresh_masks = [fresh_bias[r] for r in range(ROWS)]
    scale = WIDTH ** (-0.5)
    scores = dot_t(query, keys) * scale + jnp.concatenate(masks, axis=0)
    fresh = dot_t(query, fresh_keys[...]) * scale + jnp.concatenate(fresh_masks, axis=0)
    peak = jnp.maximum(
        jnp.max(scores, axis=1, keepdims=True), jnp.max(fresh, axis=1, keepdims=True)
    )
    peak = jnp.maximum(peak, floor).astype(bf16).astype(f32)
    weights = jnp.exp(scores - peak).astype(bf16)
    fresh_weights = jnp.exp(fresh - peak).astype(bf16)
    summed = dot(weights, values) + dot(fresh_weights, fresh_v)
    total = summed[:, WIDTH:]
    mean = summed[:, :WIDTH] / jnp.where(total > 0.0, total, 1.0)
    hi, rest = split(total)
    lane = iota(total.shape, 1)
    stat = jnp.where(lane == 0, peak, jnp.where(lane == 1, hi, rest))
    for r in range(ROWS):
        block[:, r, :] = mean[r * each : (r + 1) * each]
        block[:, ROWS + r, :] = stat[r * each : (r + 1) * each]
    out[...] = block[...].astype(bf16)


def finish(got, out):
    n = got.shape[0]
    parts = got[...].astype(f32)
    flat = parts.reshape(n * 8, WIDTH)
    lane = iota(flat.shape, 1)
    ones = jnp.ones((WIDTH, WIDTH), bf16)
    peaks = dot(jnp.where(lane == 0, flat, 0.0).astype(bf16), ones).reshape(n, 8, WIDTH)
    totals = jnp.where((lane == 1) | (lane == 2), flat, 0.0).astype(bf16)
    totals = dot(totals, ones).reshape(n, 8, WIDTH)
    factors = jnp.exp(peaks - jnp.max(peaks, axis=0)[None]) * totals
    factors = pltpu.roll(factors, ROWS, 1)
    mean = jnp.sum(factors * parts, axis=0) / jnp.sum(factors, axis=0)
    out[...] = jnp.broadcast_to(mean[:ROWS].astype(bf16)[None], out.shape)


def project(attended, weight, out):
    rows = jnp.concatenate([attended[:, r, :].astype(f32) for r in range(ROWS)], axis=0)
    shape = (GROUP * COUNT, GROUP * COUNT)
    to, of = iota(shape, 0), iota(shape, 1)
    move = (to // COUNT == (of // STEPS) % GROUP) & (to % ROWS == of // (GROUP * STEPS))
    move = move & ((to // ROWS) % STEPS == of % STEPS)
    moved = dot(jnp.where(move, 1.0, 0.0).astype(bf16), rows.astype(bf16)).astype(bf16)
    features = jnp.concatenate(
        [moved[COUNT * g : COUNT * (g + 1), :] for g in range(GROUP)], axis=1
    )
    out[...] = jnp.broadcast_to(dot(features, weight[...]).astype(bf16)[None], out.shape)


def normalise(parts, stream_in, gain, out, stream_out, rows):
    for i in range(STEPS):
        rows[ROWS * i : ROWS * (i + 1), :] = stream_in[i]
    stream = rows[...] + jnp.sum(parts[...].astype(f32), axis=0)
    for i in range(STEPS):
        stream_out[i] = stream[ROWS * i : ROWS * (i + 1)]
    squares = jnp.sum(stream * stream, axis=1, keepdims=True)
    hi, rest = split(squares)
    mid, rest = split(rest)
    at = iota((COUNT, WIDTH), 1) - iota((COUNT, WIDTH), 0)
    stat = jnp.where(at == 0, hi, jnp.where(at == 32, mid, jnp.where(at == 64, rest, 0.0)))
    stat = jnp.broadcast_to(jnp.sum(stat, axis=0, keepdims=True), (8, WIDTH))
    scaled = stream * gain[...]
    block = jnp.concatenate([scaled[:, :WIDTH], scaled[:, WIDTH:], stat], axis=0).astype(bf16)
    out[...] = jnp.broadcast_to(block[None], out.shape)


def feed(got, weight, out):
    n = got.shape[0]
    tokens = jnp.concatenate(
        [got[s, COUNT * j : COUNT * (j + 1), :] for s in range(n) for j in range(2)], axis=1
    )
    stats = jnp.sum(got[:, 32:40, :].astype(f32), axis=0)
    stats = jnp.concatenate([stats, stats], axis=0)
    at = iota((COUNT, WIDTH), 1) - iota((COUNT, WIDTH), 0)
    stats = jnp.where((at == 0) | (at == 32) | (at == 64), stats, 0.0)
    squares = jnp.sum(stats, axis=1, keepdims=True)
    inverse = lax.rsqrt(squares / (n * 2 * WIDTH) + epsilon)
    gate = dot_t(tokens, weight[0]) * inverse
    up = dot_t(tokens, weight[1]) * inverse
    hidden = gate / (1.0 + jnp.exp(-gate)) * up
    for i in range(STEPS):
        out[i] = hidden[ROWS * i : ROWS * (i + 1)].astype(bf16)


def send(x, axis):
    return lax.all_to_all(x, axis, split_axis=0, concat_axis=0, tiled=True)


def shards(
    queries,
    drafted_key_value,
    paged_key_value,
    block_table,
    page_count,
    tail_fill,
    out_weight,
    stream_in,
    norm_gain,
    gate_up,
):
    seq_index = lax.axis_index(("z", "y"))
    seq_count = lax.axis_size(("z", "y"))
    pages, page_len = paged_key_value.shape[2], paged_key_value.shape[3]
    columns = out_weight.shape[1]
    units = gate_up.shape[1]

    shape = jax.ShapeDtypeStruct
    dma = pltpu.SemaphoreType.DMA
    mine = call(copies, shape((seq_count, STEPS, ROWS * QUARTER), bf16), "v")(queries)
    gathered = send(mine, ("z", "y"))

    drafted = drafted_key_value.transpose(0, 1, 3, 2, 4).reshape(COUNT, 2, WIDTH)
    table = call(tie, shape(block_table.shape, jnp.int32), "vh", limit=62 * 2**20)(
        block_table, gate_up
    )
    bias, fresh_bias, fresh_keys, fresh_values, held = call(
        prepare,
        (
            shape((ROWS, pages * page_len), f32),
            shape((ROWS, GROUP * STEPS, COUNT), f32),
            shape((COUNT, WIDTH), bf16),
            shape((COUNT, WIDTH), bf16),
            shape(paged_key_value.shape, bf16),
        ),
        "vsssvh",
        [dma((1,))],
        limit=8 * 2**20,
    )(table, page_count, tail_fill, seq_index.reshape(1), drafted, paged_key_value)
    block = call(
        attend,
        shape((seq_count, 2 * ROWS, WIDTH), bf16),
        "vvvvvv",
        [pltpu.VMEM((seq_count, 2 * ROWS, WIDTH), f32)],
    )(gathered, held, fresh_keys, fresh_values, bias, fresh_bias)
    attended = call(finish, shape((seq_count, ROWS, WIDTH), bf16), "v")(
        send(block, ("z", "y"))
    )
    partial_sum = call(project, shape((SIDE, COUNT, columns), bf16), "vv")(
        send(attended, ("z", "y")), out_weight
    )
    scaled, stream = call(
        normalise,
        (shape((seq_count, 40, WIDTH), bf16), shape((STEPS, ROWS, columns), f32)),
        "vvv",
        [pltpu.VMEM((COUNT, columns), f32)],
    )(send(partial_sum, ("x", "core")), stream_in, norm_gain.reshape(1, columns))
    hidden = call(feed, shape((STEPS, ROWS, units), bf16), "vv")(
        send(scaled, ("z", "y")), gate_up
    )
    return hidden, stream


def solution(mesh):
    fine = Mesh(mesh.devices.reshape(4, 2, 8, 8), ("x", "core", "z", "y"))
    kvh, seq = ("x", "core"), ("z", "y")
    placed = (
        P(None, None, kvh + seq),
        P(None, None, None, kvh, None),
        P(None, kvh, seq, None, None),
        P(),
        P(),
        P(),
        P(kvh, seq),
        P(None, None, seq),
        P(seq),
        P(None, kvh + seq, None),
    )
    return jax.shard_map(
        shards,
        mesh=fine,
        in_specs=placed,
        out_specs=(P(None, None, kvh + seq), P(None, None, seq)),
        check_vma=False,
    )
```

```python
import jax
import jax.numpy as jnp
from jax import lax
from jax.experimental import pallas as pl
from jax.experimental.pallas import tpu as pltpu
from jax.sharding import Mesh
from jax.sharding import PartitionSpec as P

QUERY_HEADS = 128
KEY_VALUE_HEADS = 8
GROUP = QUERY_HEADS // KEY_VALUE_HEADS
WIDTH = 128
STEPS = 4
ROWS = 4
COUNT = STEPS * ROWS
QUARTER = 32
SIDE = 8

low = -1e30
floor = -1e29
epsilon = 1e-05
f32 = jnp.float32
bf16 = jnp.bfloat16


def iota(shape, axis):
    return lax.broadcasted_iota(jnp.int32, shape, axis)


def dot(a, b):
    return lax.dot_general(a, b, (((1,), (0,)), ((), ())), preferred_element_type=f32)


def dot_t(a, b):
    return lax.dot_general(a, b, (((1,), (1,)), ((), ())), preferred_element_type=f32)


def split(x):
    hi = x.astype(bf16).astype(f32)
    return hi, x - hi


def call(body, out_shape, inputs="", scratch=(), limit=32 * 2**20, moved=2**24):
    spaces = {"v": pltpu.VMEM, "h": pl.ANY, "s": pltpu.SMEM}
    return pl.pallas_call(
        body,
        out_shape=out_shape,
        in_specs=[pl.BlockSpec(memory_space=spaces[c]) for c in inputs],
        scratch_shapes=list(scratch),
        cost_estimate=pl.CostEstimate(flops=2**26, bytes_accessed=moved, transcendentals=2**18),
        compiler_params=pltpu.CompilerParams(vmem_limit_bytes=limit),
    )


def begin(pairs, sems):
    moves = [pltpu.make_async_copy(a, b, sems.at[i]) for i, (a, b) in enumerate(pairs)]
    for move in moves:
        move.start()
    return moves


def copies(queries, out):
    x = queries[...].astype(f32)
    x = jnp.concatenate([x[:, r, :] for r in range(ROWS)], axis=1).astype(bf16)
    out[...] = jnp.broadcast_to(x[None], out.shape)


def prepare(
    table, count, tail, index, drafted, paged, bias, fresh_bias, fresh_keys, fresh_values, held, sems
):
    moves = begin([(paged, held)], sems)
    pages, page_len = paged.shape[2], paged.shape[3]
    row, page = iota(table.shape, 0), iota(table.shape, 1)
    counts = tails = jnp.zeros(table.shape, jnp.int32)
    for r in range(ROWS):
        counts = jnp.where(row == r, count[r], counts)
        tails = jnp.where(row == r, tail[r], tails)
    fill = jnp.where(page == counts - 1, tails, page_len).astype(f32)
    fill = jnp.where(page < counts, fill, 0.0)
    slots = table[...]
    token = iota((ROWS, page_len), 1).astype(f32)
    for p in range(pages):
        filled = jnp.where(slots == index[0] * pages + p, fill, 0.0)
        filled = jnp.max(filled, axis=1, keepdims=True)
        bias[:, p * page_len : (p + 1) * page_len] = jnp.where(token < filled, 0.0, low)
    step = iota((GROUP * STEPS, COUNT), 0) % STEPS
    key = iota((GROUP * STEPS, COUNT), 1)
    causal = key // ROWS <= step
    for r in range(ROWS):
        ok = causal & (key % ROWS == r) & (index[0] == r)
        fresh_bias[r] = jnp.where(ok, 0.0, low)
    both = drafted[...].astype(f32)
    fresh_keys[...] = both[:, 0, :].astype(bf16)
    fresh_values[...] = both[:, 1, :].astype(bf16)
    moves[0].wait()


def attend(
    gathered,
    paged,
    fresh_keys,
    fresh_values,
    bias,
    fresh_bias,
    out,
    block,
):
    sent = jnp.concatenate([gathered[:, i, :].astype(f32) for i in range(STEPS)], axis=0)
    shape = (STEPS * GROUP * 4, WIDTH)
    quarter = iota(shape, 0) % 4
    diagonal = iota(shape, 1) // QUARTER == quarter
    turned = [sent] + [pltpu.roll(sent, QUARTER * d, 1) for d in range(1, 4)]
    pick_row = iota((GROUP * STEPS, shape[0]), 0)
    pick_col = iota((GROUP * STEPS, shape[0]), 1)
    pick = (pick_row // STEPS == (pick_col // 4) % GROUP) & (
        pick_row % STEPS == pick_col // (4 * GROUP)
    )
    pick = jnp.where(pick, 1.0, 0.0).astype(bf16)
    placed = []
    for r in range(ROWS):
        chosen = turned[(3 - r) % 4]
        for c in range(3):
            chosen = jnp.where(quarter == c, turned[(c - r) % 4], chosen)
        placed.append(jnp.where(diagonal, chosen, 0.0).astype(bf16))
    query = dot(pick, jnp.concatenate(placed, axis=1)).astype(bf16)
    query = jnp.concatenate([query[:, r * WIDTH : (r + 1) * WIDTH] for r in range(ROWS)], axis=0)
    keys = paged[0, 0].reshape(-1, WIDTH)
    values = paged[1, 0].reshape(-1, WIDTH)
    values = jnp.concatenate([values, jnp.ones(values.shape, bf16)], axis=1)
    fresh_v = fresh_values[...]
    fresh_v = jnp.concatenate([fresh_v, jnp.ones(fresh_v.shape, bf16)], axis=1)
    each = GROUP * STEPS
    masks = [jnp.broadcast_to(bias[r : r + 1, :], (each, bias.shape[1])) for r in range(ROWS)]
    fresh_masks = [fresh_bias[r] for r in range(ROWS)]
    scale = WIDTH ** (-0.5)
    scores = dot_t(query, keys) * scale + jnp.concatenate(masks, axis=0)
    fresh = dot_t(query, fresh_keys[...]) * scale + jnp.concatenate(fresh_masks, axis=0)
    peak = jnp.maximum(
        jnp.max(scores, axis=1, keepdims=True), jnp.max(fresh, axis=1, keepdims=True)
    )
    peak = jnp.maximum(peak, floor).astype(bf16).astype(f32)
    weights = jnp.exp(scores - peak).astype(bf16)
    fresh_weights = jnp.exp(fresh - peak).astype(bf16)
    summed = dot(weights, values) + dot(fresh_weights, fresh_v)
    total = summed[:, WIDTH:]
    mean = summed[:, :WIDTH] / jnp.where(total > 0.0, total, 1.0)
    hi, rest = split(total)
    lane = iota(total.shape, 1)
    stat = jnp.where(lane == 0, peak, jnp.where(lane == 1, hi, rest))
    for r in range(ROWS):
        block[:, r, :] = mean[r * each : (r + 1) * each]
        block[:, ROWS + r, :] = stat[r * each : (r + 1) * each]
    out[...] = block[...].astype(bf16)


def finish(got, gate_up, out):
    n = got.shape[0]
    parts = got[...].astype(f32)
    flat = parts.reshape(n * 8, WIDTH)
    lane = iota(flat.shape, 1)
    ones = jnp.ones((WIDTH, WIDTH), bf16)
    peaks = dot(jnp.where(lane == 0, flat, 0.0).astype(bf16), ones).reshape(n, 8, WIDTH)
    totals = jnp.where((lane == 1) | (lane == 2), flat, 0.0).astype(bf16)
    totals = dot(totals, ones).reshape(n, 8, WIDTH)
    factors = jnp.exp(peaks - jnp.max(peaks, axis=0)[None]) * totals
    factors = pltpu.roll(factors, ROWS, 1)
    mean = jnp.sum(factors * parts, axis=0) / jnp.sum(factors, axis=0)
    out[...] = jnp.broadcast_to(mean[:ROWS].astype(bf16)[None], out.shape)


def project(attended, weight, out):
    rows = jnp.concatenate([attended[:, r, :].astype(f32) for r in range(ROWS)], axis=0)
    shape = (GROUP * COUNT, GROUP * COUNT)
    to, of = iota(shape, 0), iota(shape, 1)
    move = (to // COUNT == (of // STEPS) % GROUP) & (to % ROWS == of // (GROUP * STEPS))
    move = move & ((to // ROWS) % STEPS == of % STEPS)
    moved = dot(jnp.where(move, 1.0, 0.0).astype(bf16), rows.astype(bf16)).astype(bf16)
    features = jnp.concatenate(
        [moved[COUNT * g : COUNT * (g + 1), :] for g in range(GROUP)], axis=1
    )
    out[...] = jnp.broadcast_to(dot(features, weight[...]).astype(bf16)[None], out.shape)


def normalise(parts, stream_in, gain, out, stream_out, rows):
    for i in range(STEPS):
        rows[ROWS * i : ROWS * (i + 1), :] = stream_in[i]
    stream = rows[...] + jnp.sum(parts[...].astype(f32), axis=0)
    for i in range(STEPS):
        stream_out[i] = stream[ROWS * i : ROWS * (i + 1)]
    squares = jnp.sum(stream * stream, axis=1, keepdims=True)
    hi, rest = split(squares)
    mid, rest = split(rest)
    at = iota((COUNT, WIDTH), 1) - iota((COUNT, WIDTH), 0)
    stat = jnp.where(at == 0, hi, jnp.where(at == 32, mid, jnp.where(at == 64, rest, 0.0)))
    stat = jnp.broadcast_to(jnp.sum(stat, axis=0, keepdims=True), (8, WIDTH))
    scaled = stream * gain[...]
    block = jnp.concatenate([scaled[:, :WIDTH], scaled[:, WIDTH:], stat], axis=0).astype(bf16)
    out[...] = jnp.broadcast_to(block[None], out.shape)


def feed(got, weight, out):
    n = got.shape[0]
    tokens = jnp.concatenate(
        [got[s, COUNT * j : COUNT * (j + 1), :] for s in range(n) for j in range(2)], axis=1
    )
    stats = jnp.sum(got[:, 32:40, :].astype(f32), axis=0)
    stats = jnp.concatenate([stats, stats], axis=0)
    at = iota((COUNT, WIDTH), 1) - iota((COUNT, WIDTH), 0)
    stats = jnp.where((at == 0) | (at == 32) | (at == 64), stats, 0.0)
    squares = jnp.sum(stats, axis=1, keepdims=True)
    inverse = lax.rsqrt(squares / (n * 2 * WIDTH) + epsilon)
    gate = dot_t(tokens, weight[0]) * inverse
    up = dot_t(tokens, weight[1]) * inverse
    hidden = gate / (1.0 + jnp.exp(-gate)) * up
    for i in range(STEPS):
        out[i] = hidden[ROWS * i : ROWS * (i + 1)].astype(bf16)


def send(x, axis):
    return lax.all_to_all(x, axis, split_axis=0, concat_axis=0, tiled=True)


def shards(
    queries,
    drafted_key_value,
    paged_key_value,
    block_table,
    page_count,
    tail_fill,
    out_weight,
    stream_in,
    norm_gain,
    gate_up,
):
    seq_index = lax.axis_index(("z", "y"))
    seq_count = lax.axis_size(("z", "y"))
    pages, page_len = paged_key_value.shape[2], paged_key_value.shape[3]
    columns = out_weight.shape[1]
    units = gate_up.shape[1]

    shape = jax.ShapeDtypeStruct
    dma = pltpu.SemaphoreType.DMA
    mine = call(copies, shape((seq_count, STEPS, ROWS * QUARTER), bf16), "v")(queries)
    gathered = send(mine, ("z", "y"))

    drafted = drafted_key_value.transpose(0, 1, 3, 2, 4).reshape(COUNT, 2, WIDTH)
    bias, fresh_bias, fresh_keys, fresh_values, held = call(
        prepare,
        (
            shape((ROWS, pages * page_len), f32),
            shape((ROWS, GROUP * STEPS, COUNT), f32),
            shape((COUNT, WIDTH), bf16),
            shape((COUNT, WIDTH), bf16),
            shape(paged_key_value.shape, bf16),
        ),
        "vsssvh",
        [dma((1,))],
        limit=8 * 2**20,
    )(block_table, page_count, tail_fill, seq_index.reshape(1), drafted, paged_key_value)
    block = call(
        attend,
        shape((seq_count, 2 * ROWS, WIDTH), bf16),
        "vvvvvv",
        [pltpu.VMEM((seq_count, 2 * ROWS, WIDTH), f32)],
    )(gathered, held, fresh_keys, fresh_values, bias, fresh_bias)
    attended = call(
        finish, shape((seq_count, ROWS, WIDTH), bf16), "vh", limit=63_600_000
    )(send(block, ("z", "y")), gate_up)
    partial_sum = call(project, shape((SIDE, COUNT, columns), bf16), "vv")(
        send(attended, ("z", "y")), out_weight
    )
    scaled, stream = call(
        normalise,
        (shape((seq_count, 40, WIDTH), bf16), shape((STEPS, ROWS, columns), f32)),
        "vvv",
        [pltpu.VMEM((COUNT, columns), f32)],
    )(send(partial_sum, ("x", "core")), stream_in, norm_gain.reshape(1, columns))
    hidden = call(feed, shape((STEPS, ROWS, units), bf16), "vv")(
        send(scaled, ("z", "y")), gate_up
    )
    return hidden, stream


def solution(mesh):
    fine = Mesh(mesh.devices.reshape(4, 2, 8, 8), ("x", "core", "z", "y"))
    kvh, seq = ("x", "core"), ("z", "y")
    placed = (
        P(None, None, kvh + seq),
        P(None, None, None, kvh, None),
        P(None, kvh, seq, None, None),
        P(),
        P(),
        P(),
        P(kvh, seq),
        P(None, None, seq),
        P(seq),
        P(None, kvh + seq, None),
    )
    return jax.shard_map(
        shards,
        mesh=fine,
        in_specs=placed,
        out_specs=(P(None, None, kvh + seq), P(None, None, seq)),
        check_vma=False,
    )
```

```python
import jax
import jax.numpy as jnp
from jax import lax
from jax.experimental import pallas as pl
from jax.experimental.pallas import tpu as pltpu
from jax.sharding import Mesh
from jax.sharding import PartitionSpec as P

QUERY_HEADS = 128
KEY_VALUE_HEADS = 8
GROUP = QUERY_HEADS // KEY_VALUE_HEADS
WIDTH = 128
STEPS = 4
ROWS = 4
COUNT = STEPS * ROWS
QUARTER = 32
PAGES = 8
SIDE = 8

low = -1e30
floor = -1e29
epsilon = 1e-05
f32 = jnp.float32
bf16 = jnp.bfloat16


def iota(shape, axis):
    return lax.broadcasted_iota(jnp.int32, shape, axis)


def dot(a, b):
    return lax.dot_general(a, b, (((1,), (0,)), ((), ())), preferred_element_type=f32)


def dot_t(a, b):
    return lax.dot_general(a, b, (((1,), (1,)), ((), ())), preferred_element_type=f32)


def split(x):
    hi = x.astype(bf16).astype(f32)
    return hi, x - hi


def call(body, out_shape, inputs="", scratch=(), limit=32 * 2**20, moved=2**24):
    spaces = {"v": pltpu.VMEM, "h": pl.ANY, "s": pltpu.SMEM}
    return pl.pallas_call(
        body,
        out_shape=out_shape,
        in_specs=[pl.BlockSpec(memory_space=spaces[c]) for c in inputs],
        scratch_shapes=list(scratch),
        cost_estimate=pl.CostEstimate(flops=2**26, bytes_accessed=moved, transcendentals=2**18),
        compiler_params=pltpu.CompilerParams(vmem_limit_bytes=limit),
    )


def begin(pairs, sems):
    moves = [pltpu.make_async_copy(a, b, sems.at[i]) for i, (a, b) in enumerate(pairs)]
    for move in moves:
        move.start()
    return moves


def copies(queries, out):
    x = queries[...].astype(f32)
    x = jnp.concatenate([x[:, r, :] for r in range(ROWS)], axis=1).astype(bf16)
    out[...] = jnp.broadcast_to(x[None], out.shape)


def prepare(table, count, tail, index, drafted, bias, fresh_keys, fresh_values):
    pages = PAGES
    page_len = bias.shape[1] // pages
    row, page = iota(table.shape, 0), iota(table.shape, 1)
    counts = tails = jnp.zeros(table.shape, jnp.int32)
    for r in range(ROWS):
        counts = jnp.where(row == r, count[r], counts)
        tails = jnp.where(row == r, tail[r], tails)
    fill = jnp.where(page == counts - 1, tails, page_len).astype(f32)
    fill = jnp.where(page < counts, fill, 0.0)
    slots = table[...]
    token = iota((ROWS, page_len), 1).astype(f32)
    for p in range(pages):
        filled = jnp.where(slots == index[0] * pages + p, fill, 0.0)
        filled = jnp.max(filled, axis=1, keepdims=True)
        bias[:, p * page_len : (p + 1) * page_len] = jnp.where(token < filled, 0.0, low)
    both = drafted[...].astype(f32)
    fresh_keys[...] = both[:, 0, :].astype(bf16)
    fresh_values[...] = both[:, 1, :].astype(bf16)


def attend(gathered, paged, fresh_keys, fresh_values, bias, index, out, block):
    sent = jnp.concatenate([gathered[:, i, :].astype(f32) for i in range(STEPS)], axis=0)
    shape = (STEPS * GROUP * 4, WIDTH)
    quarter = iota(shape, 0) % 4
    diagonal = iota(shape, 1) // QUARTER == quarter
    turned = [sent] + [pltpu.roll(sent, QUARTER * d, 1) for d in range(1, 4)]
    pick_row = iota((GROUP * STEPS, shape[0]), 0)
    pick_col = iota((GROUP * STEPS, shape[0]), 1)
    pick = (pick_row // STEPS == (pick_col // 4) % GROUP) & (
        pick_row % STEPS == pick_col // (4 * GROUP)
    )
    pick = jnp.where(pick, 1.0, 0.0).astype(bf16)
    placed = []
    for r in range(ROWS):
        chosen = turned[(3 - r) % 4]
        for c in range(3):
            chosen = jnp.where(quarter == c, turned[(c - r) % 4], chosen)
        placed.append(jnp.where(diagonal, chosen, 0.0).astype(bf16))
    query = dot(pick, jnp.concatenate(placed, axis=1)).astype(bf16)
    query = jnp.concatenate([query[:, r * WIDTH : (r + 1) * WIDTH] for r in range(ROWS)], axis=0)
    keys = paged[0, 0].reshape(-1, WIDTH)
    values = paged[1, 0].reshape(-1, WIDTH)
    values = jnp.concatenate([values, jnp.ones(values.shape, bf16)], axis=1)
    fresh_v = fresh_values[...]
    fresh_v = jnp.concatenate([fresh_v, jnp.ones(fresh_v.shape, bf16)], axis=1)
    each = GROUP * STEPS
    masks = [jnp.broadcast_to(bias[r : r + 1, :], (each, bias.shape[1])) for r in range(ROWS)]
    query_at, key_at = iota((ROWS * each, COUNT), 0), iota((ROWS * each, COUNT), 1)
    ok = (key_at % ROWS == query_at // each) & (key_at // ROWS <= query_at % STEPS)
    ok = ok & (query_at // each == index[0])
    scale = WIDTH ** (-0.5)
    scores = dot_t(query, keys) * scale + jnp.concatenate(masks, axis=0)
    fresh = jnp.where(ok, dot_t(query, fresh_keys[...]) * scale, low)
    peak = jnp.maximum(
        jnp.max(scores, axis=1, keepdims=True), jnp.max(fresh, axis=1, keepdims=True)
    )
    peak = jnp.maximum(peak, floor).astype(bf16).astype(f32)
    weights = jnp.exp(scores - peak).astype(bf16)
    fresh_weights = jnp.exp(fresh - peak).astype(bf16)
    summed = dot(weights, values) + dot(fresh_weights, fresh_v)
    total = summed[:, WIDTH:]
    mean = summed[:, :WIDTH] / jnp.where(total > 0.0, total, 1.0)
    hi, rest = split(total)
    lane = iota(total.shape, 1)
    stat = jnp.where(lane == 0, peak, jnp.where(lane == 1, hi, rest))
    for r in range(ROWS):
        block[:, r, :] = mean[r * each : (r + 1) * each]
        block[:, ROWS + r, :] = stat[r * each : (r + 1) * each]
    out[...] = block[...].astype(bf16)


def finish(got, out):
    n = got.shape[0]
    parts = got[...].astype(f32)
    flat = parts.reshape(n * 8, WIDTH)
    lane = iota(flat.shape, 1)
    ones = jnp.ones((WIDTH, WIDTH), bf16)
    peaks = dot(jnp.where(lane == 0, flat, 0.0).astype(bf16), ones).reshape(n, 8, WIDTH)
    totals = jnp.where((lane == 1) | (lane == 2), flat, 0.0).astype(bf16)
    totals = dot(totals, ones).reshape(n, 8, WIDTH)
    factors = jnp.exp(peaks - jnp.max(peaks, axis=0)[None]) * totals
    factors = pltpu.roll(factors, ROWS, 1)
    mean = jnp.sum(factors * parts, axis=0) / jnp.sum(factors, axis=0)
    out[...] = jnp.broadcast_to(mean[:ROWS].astype(bf16)[None], out.shape)


def project(attended, weight, out):
    rows = jnp.concatenate([attended[:, r, :].astype(f32) for r in range(ROWS)], axis=0)
    shape = (GROUP * COUNT, GROUP * COUNT)
    to, of = iota(shape, 0), iota(shape, 1)
    move = (to // COUNT == (of // STEPS) % GROUP) & (to % ROWS == of // (GROUP * STEPS))
    move = move & ((to // ROWS) % STEPS == of % STEPS)
    moved = dot(jnp.where(move, 1.0, 0.0).astype(bf16), rows.astype(bf16)).astype(bf16)
    features = jnp.concatenate(
        [moved[COUNT * g : COUNT * (g + 1), :] for g in range(GROUP)], axis=1
    )
    out[...] = jnp.broadcast_to(dot(features, weight[...]).astype(bf16)[None], out.shape)


def normalise(parts, stream_in, gain, out, stream_out, rows):
    for i in range(STEPS):
        rows[ROWS * i : ROWS * (i + 1), :] = stream_in[i]
    stream = rows[...] + jnp.sum(parts[...].astype(f32), axis=0)
    for i in range(STEPS):
        stream_out[i] = stream[ROWS * i : ROWS * (i + 1)]
    squares = jnp.sum(stream * stream, axis=1, keepdims=True)
    hi, rest = split(squares)
    mid, rest = split(rest)
    at = iota((COUNT, WIDTH), 1) - iota((COUNT, WIDTH), 0)
    stat = jnp.where(at == 0, hi, jnp.where(at == 32, mid, jnp.where(at == 64, rest, 0.0)))
    stat = jnp.broadcast_to(jnp.sum(stat, axis=0, keepdims=True), (8, WIDTH))
    scaled = stream * gain[...]
    block = jnp.concatenate([scaled[:, :WIDTH], scaled[:, WIDTH:], stat], axis=0).astype(bf16)
    out[...] = jnp.broadcast_to(block[None], out.shape)


def lay(got, tokens, inverse):
    n = got.shape[0]
    for s in range(n):
        for j in range(2):
            at = (2 * s + j) * WIDTH
            tokens[:, at : at + WIDTH] = got[s, COUNT * j : COUNT * (j + 1), :]
    stats = jnp.sum(got[:, 32:40, :].astype(f32), axis=0)
    stats = jnp.concatenate([stats, stats], axis=0)
    at = iota((COUNT, WIDTH), 1) - iota((COUNT, WIDTH), 0)
    stats = jnp.where((at == 0) | (at == 32) | (at == 64), stats, 0.0)
    squares = jnp.sum(stats, axis=1, keepdims=True)
    inverse[...] = jnp.broadcast_to(
        lax.rsqrt(squares / (n * 2 * WIDTH) + epsilon), inverse.shape
    )


def send(x, axis):
    return lax.all_to_all(x, axis, split_axis=0, concat_axis=0, tiled=True)


def shards(
    queries,
    drafted_key_value,
    paged_key_value,
    block_table,
    page_count,
    tail_fill,
    out_weight,
    stream_in,
    norm_gain,
    gate_up,
):
    seq_index = lax.axis_index(("z", "y"))
    seq_count = lax.axis_size(("z", "y"))
    pages, page_len = paged_key_value.shape[2], paged_key_value.shape[3]
    columns = out_weight.shape[1]
    units = gate_up.shape[1]

    shape = jax.ShapeDtypeStruct
    dma = pltpu.SemaphoreType.DMA
    mine = call(copies, shape((seq_count, STEPS, ROWS * QUARTER), bf16), "v")(queries)
    gathered = send(mine, ("z", "y"))

    drafted = drafted_key_value.transpose(0, 1, 3, 2, 4).reshape(COUNT, 2, WIDTH)
    index = seq_index.reshape(1)
    bias, fresh_keys, fresh_values = call(
        prepare,
        (
            shape((ROWS, pages * page_len), f32),
            shape((COUNT, WIDTH), bf16),
            shape((COUNT, WIDTH), bf16),
        ),
        "vsssv",
        limit=8 * 2**20,
    )(block_table, page_count, tail_fill, index, drafted)
    block = call(
        attend,
        shape((seq_count, 2 * ROWS, WIDTH), bf16),
        "vvvvvs",
        [pltpu.VMEM((seq_count, 2 * ROWS, WIDTH), f32)],
    )(gathered, paged_key_value, fresh_keys, fresh_values, bias, index)
    attended = call(finish, shape((seq_count, ROWS, WIDTH), bf16), "v")(
        send(block, ("z", "y"))
    )
    partial_sum = call(project, shape((SIDE, COUNT, columns), bf16), "vv")(
        send(attended, ("z", "y")), out_weight
    )
    scaled, stream = call(
        normalise,
        (shape((seq_count, 40, WIDTH), bf16), shape((STEPS, ROWS, columns), f32)),
        "vvv",
        [pltpu.VMEM((COUNT, columns), f32)],
    )(send(partial_sum, ("x", "core")), stream_in, norm_gain.reshape(1, columns))
    tokens, inverse = call(
        lay,
        (shape((COUNT, seq_count * columns), bf16), shape((COUNT, WIDTH), f32)),
        "v",
    )(send(scaled, ("z", "y")))
    both = jnp.einsum("nc,kfc->knf", tokens, gate_up, preferred_element_type=f32)
    both = both * inverse[None, :, :units]
    hidden = both[0] / (1.0 + jnp.exp(-both[0])) * both[1]
    hidden = hidden.astype(bf16).reshape(STEPS, ROWS, units)
    return hidden, stream


def solution(mesh):
    fine = Mesh(mesh.devices.reshape(4, 2, 8, 8), ("x", "core", "z", "y"))
    kvh, seq = ("x", "core"), ("z", "y")
    placed = (
        P(None, None, kvh + seq),
        P(None, None, None, kvh, None),
        P(None, kvh, seq, None, None),
        P(),
        P(),
        P(),
        P(kvh, seq),
        P(None, None, seq),
        P(seq),
        P(None, kvh + seq, None),
    )
    return jax.shard_map(
        shards,
        mesh=fine,
        in_specs=placed,
        out_specs=(P(None, None, kvh + seq), P(None, None, seq)),
        check_vma=False,
    )
```

```python
import jax
import jax.numpy as jnp
from jax import lax
from jax.experimental import pallas as pl
from jax.experimental.pallas import tpu as pltpu
from jax.sharding import Mesh
from jax.sharding import PartitionSpec as P

QUERY_HEADS = 128
KEY_VALUE_HEADS = 8
GROUP = QUERY_HEADS // KEY_VALUE_HEADS
WIDTH = 128
STEPS = 4
ROWS = 4
COUNT = STEPS * ROWS
QUARTER = 32
PAGES = 8
SIDE = 8

low = -1e30
floor = -1e29
epsilon = 1e-05
f32 = jnp.float32
bf16 = jnp.bfloat16


def iota(shape, axis):
    return lax.broadcasted_iota(jnp.int32, shape, axis)


def dot(a, b):
    return lax.dot_general(a, b, (((1,), (0,)), ((), ())), preferred_element_type=f32)


def dot_t(a, b):
    return lax.dot_general(a, b, (((1,), (1,)), ((), ())), preferred_element_type=f32)


def split(x):
    hi = x.astype(bf16).astype(f32)
    return hi, x - hi


def call(body, out_shape, inputs="", scratch=(), limit=32 * 2**20, moved=2**24):
    spaces = {"v": pltpu.VMEM, "h": pl.ANY, "s": pltpu.SMEM}
    return pl.pallas_call(
        body,
        out_shape=out_shape,
        in_specs=[pl.BlockSpec(memory_space=spaces[c]) for c in inputs],
        scratch_shapes=list(scratch),
        cost_estimate=pl.CostEstimate(flops=2**26, bytes_accessed=moved, transcendentals=2**18),
        compiler_params=pltpu.CompilerParams(vmem_limit_bytes=limit),
    )


def copies(queries, out):
    x = queries[...].astype(f32)
    x = jnp.concatenate([x[:, r, :] for r in range(ROWS)], axis=1).astype(bf16)
    out[...] = jnp.broadcast_to(x[None], out.shape)


def prepare(table, count, tail, index, drafted, bias, fresh_keys, fresh_values):
    pages = PAGES
    page_len = bias.shape[1] // pages
    row, page = iota(table.shape, 0), iota(table.shape, 1)
    counts = tails = jnp.zeros(table.shape, jnp.int32)
    for r in range(ROWS):
        counts = jnp.where(row == r, count[r], counts)
        tails = jnp.where(row == r, tail[r], tails)
    fill = jnp.where(page == counts - 1, tails, page_len).astype(f32)
    fill = jnp.where(page < counts, fill, 0.0)
    slots = table[...]
    token = iota((ROWS, page_len), 1).astype(f32)
    for p in range(pages):
        filled = jnp.where(slots == index[0] * pages + p, fill, 0.0)
        filled = jnp.max(filled, axis=1, keepdims=True)
        bias[:, p * page_len : (p + 1) * page_len] = jnp.where(token < filled, 0.0, low)
    both = drafted[...].astype(f32)
    fresh_keys[...] = both[:, 0, :].astype(bf16)
    fresh_values[...] = both[:, 1, :].astype(bf16)


def attend(
    gathered, paged, fresh_keys, fresh_values, bias, index, out_weight, out, held, block, sems
):
    move = pltpu.make_async_copy(out_weight, held, sems.at[0])
    move.start()
    sent = jnp.concatenate([gathered[:, i, :].astype(f32) for i in range(STEPS)], axis=0)
    shape = (STEPS * GROUP * 4, WIDTH)
    quarter = iota(shape, 0) % 4
    diagonal = iota(shape, 1) // QUARTER == quarter
    turned = [sent] + [pltpu.roll(sent, QUARTER * d, 1) for d in range(1, 4)]
    pick_row = iota((GROUP * STEPS, shape[0]), 0)
    pick_col = iota((GROUP * STEPS, shape[0]), 1)
    pick = (pick_row // STEPS == (pick_col // 4) % GROUP) & (
        pick_row % STEPS == pick_col // (4 * GROUP)
    )
    pick = jnp.where(pick, 1.0, 0.0).astype(bf16)
    placed = []
    for r in range(ROWS):
        chosen = turned[(3 - r) % 4]
        for c in range(3):
            chosen = jnp.where(quarter == c, turned[(c - r) % 4], chosen)
        placed.append(jnp.where(diagonal, chosen, 0.0).astype(bf16))
    query = dot(pick, jnp.concatenate(placed, axis=1)).astype(bf16)
    query = jnp.concatenate([query[:, r * WIDTH : (r + 1) * WIDTH] for r in range(ROWS)], axis=0)
    keys = paged[0, 0].reshape(-1, WIDTH)
    values = paged[1, 0].reshape(-1, WIDTH)
    values = jnp.concatenate([values, jnp.ones(values.shape, bf16)], axis=1)
    fresh_v = fresh_values[...]
    fresh_v = jnp.concatenate([fresh_v, jnp.ones(fresh_v.shape, bf16)], axis=1)
    each = GROUP * STEPS
    masks = [jnp.broadcast_to(bias[r : r + 1, :], (each, bias.shape[1])) for r in range(ROWS)]
    query_at, key_at = iota((ROWS * each, COUNT), 0), iota((ROWS * each, COUNT), 1)
    ok = (key_at % ROWS == query_at // each) & (key_at // ROWS <= query_at % STEPS)
    ok = ok & (query_at // each == index[0])
    scale = WIDTH ** (-0.5)
    scores = dot_t(query, keys) * scale + jnp.concatenate(masks, axis=0)
    fresh = jnp.where(ok, dot_t(query, fresh_keys[...]) * scale, low)
    peak = jnp.maximum(
        jnp.max(scores, axis=1, keepdims=True), jnp.max(fresh, axis=1, keepdims=True)
    )
    peak = jnp.maximum(peak, floor).astype(bf16).astype(f32)
    weights = jnp.exp(scores - peak).astype(bf16)
    fresh_weights = jnp.exp(fresh - peak).astype(bf16)
    summed = dot(weights, values) + dot(fresh_weights, fresh_v)
    total = summed[:, WIDTH:]
    mean = summed[:, :WIDTH] / jnp.where(total > 0.0, total, 1.0)
    hi, rest = split(total)
    lane = iota(total.shape, 1)
    stat = jnp.where(lane == 0, peak, jnp.where(lane == 1, hi, rest))
    for r in range(ROWS):
        block[:, r, :] = mean[r * each : (r + 1) * each]
        block[:, ROWS + r, :] = stat[r * each : (r + 1) * each]
    out[...] = block[...].astype(bf16)
    move.wait()


def finish(got, out):
    n = got.shape[0]
    parts = got[...].astype(f32)
    flat = parts.reshape(n * 8, WIDTH)
    lane = iota(flat.shape, 1)
    ones = jnp.ones((WIDTH, WIDTH), bf16)
    peaks = dot(jnp.where(lane == 0, flat, 0.0).astype(bf16), ones).reshape(n, 8, WIDTH)
    totals = jnp.where((lane == 1) | (lane == 2), flat, 0.0).astype(bf16)
    totals = dot(totals, ones).reshape(n, 8, WIDTH)
    factors = jnp.exp(peaks - jnp.max(peaks, axis=0)[None]) * totals
    factors = pltpu.roll(factors, ROWS, 1)
    mean = jnp.sum(factors * parts, axis=0) / jnp.sum(factors, axis=0)
    out[...] = jnp.broadcast_to(mean[:ROWS].astype(bf16)[None], out.shape)


def project(attended, weight, out):
    rows = jnp.concatenate([attended[:, r, :].astype(f32) for r in range(ROWS)], axis=0)
    shape = (GROUP * COUNT, GROUP * COUNT)
    to, of = iota(shape, 0), iota(shape, 1)
    move = (to // COUNT == (of // STEPS) % GROUP) & (to % ROWS == of // (GROUP * STEPS))
    move = move & ((to // ROWS) % STEPS == of % STEPS)
    moved = dot(jnp.where(move, 1.0, 0.0).astype(bf16), rows.astype(bf16)).astype(bf16)
    features = jnp.concatenate(
        [moved[COUNT * g : COUNT * (g + 1), :] for g in range(GROUP)], axis=1
    )
    out[...] = jnp.broadcast_to(dot(features, weight[...]).astype(bf16)[None], out.shape)


def normalise(parts, stream_in, gain, out, stream_out, rows):
    for i in range(STEPS):
        rows[ROWS * i : ROWS * (i + 1), :] = stream_in[i]
    stream = rows[...] + jnp.sum(parts[...].astype(f32), axis=0)
    for i in range(STEPS):
        stream_out[i] = stream[ROWS * i : ROWS * (i + 1)]
    squares = jnp.sum(stream * stream, axis=1, keepdims=True)
    hi, rest = split(squares)
    mid, rest = split(rest)
    at = iota((COUNT, WIDTH), 1) - iota((COUNT, WIDTH), 0)
    stat = jnp.where(at == 0, hi, jnp.where(at == 32, mid, jnp.where(at == 64, rest, 0.0)))
    stat = jnp.broadcast_to(jnp.sum(stat, axis=0, keepdims=True), (8, WIDTH))
    scaled = stream * gain[...]
    block = jnp.concatenate([scaled[:, :WIDTH], scaled[:, WIDTH:], stat], axis=0).astype(bf16)
    out[...] = jnp.broadcast_to(block[None], out.shape)


def lay(got, tokens, inverse):
    n = got.shape[0]
    for s in range(n):
        for j in range(2):
            at = (2 * s + j) * WIDTH
            tokens[:, at : at + WIDTH] = got[s, COUNT * j : COUNT * (j + 1), :]
    stats = jnp.sum(got[:, 32:40, :].astype(f32), axis=0)
    stats = jnp.concatenate([stats, stats], axis=0)
    at = iota((COUNT, WIDTH), 1) - iota((COUNT, WIDTH), 0)
    stats = jnp.where((at == 0) | (at == 32) | (at == 64), stats, 0.0)
    squares = jnp.sum(stats, axis=1, keepdims=True)
    inverse[...] = jnp.broadcast_to(
        lax.rsqrt(squares / (n * 2 * WIDTH) + epsilon), inverse.shape
    )


def send(x, axis):
    return lax.all_to_all(x, axis, split_axis=0, concat_axis=0, tiled=True)


def shards(
    queries,
    drafted_key_value,
    paged_key_value,
    block_table,
    page_count,
    tail_fill,
    out_weight,
    stream_in,
    norm_gain,
    gate_up,
):
    seq_index = lax.axis_index(("z", "y"))
    seq_count = lax.axis_size(("z", "y"))
    pages, page_len = paged_key_value.shape[2], paged_key_value.shape[3]
    columns = out_weight.shape[1]
    units = gate_up.shape[1]

    shape = jax.ShapeDtypeStruct
    mine = call(copies, shape((seq_count, STEPS, ROWS * QUARTER), bf16), "v")(queries)
    gathered = send(mine, ("z", "y"))

    drafted = drafted_key_value.transpose(0, 1, 3, 2, 4).reshape(COUNT, 2, WIDTH)
    index = seq_index.reshape(1)
    bias, fresh_keys, fresh_values = call(
        prepare,
        (
            shape((ROWS, pages * page_len), f32),
            shape((COUNT, WIDTH), bf16),
            shape((COUNT, WIDTH), bf16),
        ),
        "vsssv",
        limit=8 * 2**20,
    )(block_table, page_count, tail_fill, index, drafted)
    block, weight = call(
        attend,
        (shape((seq_count, 2 * ROWS, WIDTH), bf16), shape(out_weight.shape, bf16)),
        "vvvvvsh",
        [pltpu.VMEM((seq_count, 2 * ROWS, WIDTH), f32), pltpu.SemaphoreType.DMA((1,))],
    )(gathered, paged_key_value, fresh_keys, fresh_values, bias, index, out_weight)
    attended = call(finish, shape((seq_count, ROWS, WIDTH), bf16), "v")(
        send(block, ("z", "y"))
    )
    partial_sum = call(project, shape((SIDE, COUNT, columns), bf16), "vv")(
        send(attended, ("z", "y")), weight
    )
    scaled, stream = call(
        normalise,
        (shape((seq_count, 40, WIDTH), bf16), shape((STEPS, ROWS, columns), f32)),
        "vvv",
        [pltpu.VMEM((COUNT, columns), f32)],
    )(send(partial_sum, ("x", "core")), stream_in, norm_gain.reshape(1, columns))
    tokens, inverse = call(
        lay,
        (shape((COUNT, seq_count * columns), bf16), shape((COUNT, WIDTH), f32)),
        "v",
    )(send(scaled, ("z", "y")))
    both = jnp.einsum("nc,kfc->knf", tokens, gate_up, preferred_element_type=f32)
    both = both * inverse[None, :, :units]
    hidden = both[0] / (1.0 + jnp.exp(-both[0])) * both[1]
    hidden = hidden.astype(bf16).reshape(STEPS, ROWS, units)
    return hidden, stream


def solution(mesh):
    fine = Mesh(mesh.devices.reshape(4, 2, 8, 8), ("x", "core", "z", "y"))
    kvh, seq = ("x", "core"), ("z", "y")
    placed = (
        P(None, None, kvh + seq),
        P(None, None, None, kvh, None),
        P(None, kvh, seq, None, None),
        P(),
        P(),
        P(),
        P(kvh, seq),
        P(None, None, seq),
        P(seq),
        P(None, kvh + seq, None),
    )
    return jax.shard_map(
        shards,
        mesh=fine,
        in_specs=placed,
        out_specs=(P(None, None, kvh + seq), P(None, None, seq)),
        check_vma=False,
    )
```

```python
import jax
import jax.numpy as jnp
from jax import lax
from jax.experimental import pallas as pl
from jax.experimental.pallas import tpu as pltpu
from jax.sharding import Mesh
from jax.sharding import PartitionSpec as P

QUERY_HEADS = 128
KEY_VALUE_HEADS = 8
GROUP = QUERY_HEADS // KEY_VALUE_HEADS
WIDTH = 128
STEPS = 4
ROWS = 4
COUNT = STEPS * ROWS
QUARTER = 32
PAGES = 8
SIDE = 8

low = -1e30
floor = -1e29
epsilon = 1e-05
f32 = jnp.float32
bf16 = jnp.bfloat16


def iota(shape, axis):
    return lax.broadcasted_iota(jnp.int32, shape, axis)


def dot(a, b):
    return lax.dot_general(a, b, (((1,), (0,)), ((), ())), preferred_element_type=f32)


def dot_t(a, b):
    return lax.dot_general(a, b, (((1,), (1,)), ((), ())), preferred_element_type=f32)


def split(x):
    hi = x.astype(bf16).astype(f32)
    return hi, x - hi


def call(body, out_shape, inputs="", scratch=(), limit=32 * 2**20, moved=2**24):
    spaces = {"v": pltpu.VMEM, "h": pl.ANY, "s": pltpu.SMEM}
    return pl.pallas_call(
        body,
        out_shape=out_shape,
        in_specs=[pl.BlockSpec(memory_space=spaces[c]) for c in inputs],
        scratch_shapes=list(scratch),
        cost_estimate=pl.CostEstimate(flops=2**26, bytes_accessed=moved, transcendentals=2**18),
        compiler_params=pltpu.CompilerParams(vmem_limit_bytes=limit),
    )


def copies(queries, out):
    x = queries[...].astype(f32)
    x = jnp.concatenate([x[:, r, :] for r in range(ROWS)], axis=1).astype(bf16)
    out[...] = jnp.broadcast_to(x[None], out.shape)


def prepare(table, count, tail, index, drafted, bias, fresh_keys, fresh_values):
    pages = PAGES
    page_len = bias.shape[1] // pages
    row, page = iota(table.shape, 0), iota(table.shape, 1)
    counts = tails = jnp.zeros(table.shape, jnp.int32)
    for r in range(ROWS):
        counts = jnp.where(row == r, count[r], counts)
        tails = jnp.where(row == r, tail[r], tails)
    fill = jnp.where(page == counts - 1, tails, page_len).astype(f32)
    fill = jnp.where(page < counts, fill, 0.0)
    slots = table[...]
    token = iota((ROWS, page_len), 1).astype(f32)
    for p in range(pages):
        filled = jnp.where(slots == index[0] * pages + p, fill, 0.0)
        filled = jnp.max(filled, axis=1, keepdims=True)
        bias[:, p * page_len : (p + 1) * page_len] = jnp.where(token < filled, 0.0, low)
    both = drafted[...].astype(f32)
    fresh_keys[...] = both[:, 0, :].astype(bf16)
    fresh_values[...] = both[:, 1, :].astype(bf16)


def attend(gathered, paged, fresh_keys, fresh_values, bias, index, out, block):
    sent = jnp.concatenate([gathered[:, i, :].astype(f32) for i in range(STEPS)], axis=0)
    shape = (STEPS * GROUP * 4, WIDTH)
    quarter = iota(shape, 0) % 4
    diagonal = iota(shape, 1) // QUARTER == quarter
    turned = [sent] + [pltpu.roll(sent, QUARTER * d, 1) for d in range(1, 4)]
    pick_row = iota((GROUP * STEPS, shape[0]), 0)
    pick_col = iota((GROUP * STEPS, shape[0]), 1)
    pick = (pick_row // STEPS == (pick_col // 4) % GROUP) & (
        pick_row % STEPS == pick_col // (4 * GROUP)
    )
    pick = jnp.where(pick, 1.0, 0.0).astype(bf16)
    placed = []
    for r in range(ROWS):
        chosen = turned[(3 - r) % 4]
        for c in range(3):
            chosen = jnp.where(quarter == c, turned[(c - r) % 4], chosen)
        placed.append(jnp.where(diagonal, chosen, 0.0).astype(bf16))
    query = dot(pick, jnp.concatenate(placed, axis=1)).astype(bf16)
    query = jnp.concatenate([query[:, r * WIDTH : (r + 1) * WIDTH] for r in range(ROWS)], axis=0)
    keys = paged[0, 0].reshape(-1, WIDTH)
    values = paged[1, 0].reshape(-1, WIDTH)
    values = jnp.concatenate([values, jnp.ones(values.shape, bf16)], axis=1)
    fresh_v = fresh_values[...]
    fresh_v = jnp.concatenate([fresh_v, jnp.ones(fresh_v.shape, bf16)], axis=1)
    each = GROUP * STEPS
    masks = [jnp.broadcast_to(bias[r : r + 1, :], (each, bias.shape[1])) for r in range(ROWS)]
    query_at, key_at = iota((ROWS * each, COUNT), 0), iota((ROWS * each, COUNT), 1)
    ok = (key_at % ROWS == query_at // each) & (key_at // ROWS <= query_at % STEPS)
    ok = ok & (query_at // each == index[0])
    scale = WIDTH ** (-0.5)
    scores = dot_t(query, keys) * scale + jnp.concatenate(masks, axis=0)
    fresh = jnp.where(ok, dot_t(query, fresh_keys[...]) * scale, low)
    peak = jnp.maximum(
        jnp.max(scores, axis=1, keepdims=True), jnp.max(fresh, axis=1, keepdims=True)
    )
    peak = jnp.maximum(peak, floor).astype(bf16).astype(f32)
    weights = jnp.exp(scores - peak).astype(bf16)
    fresh_weights = jnp.exp(fresh - peak).astype(bf16)
    summed = dot(weights, values) + dot(fresh_weights, fresh_v)
    total = summed[:, WIDTH:]
    mean = summed[:, :WIDTH] / jnp.where(total > 0.0, total, 1.0)
    hi, rest = split(total)
    lane = iota(total.shape, 1)
    stat = jnp.where(lane == 0, peak, jnp.where(lane == 1, hi, rest))
    for r in range(ROWS):
        block[:, r, :] = mean[r * each : (r + 1) * each]
        block[:, ROWS + r, :] = stat[r * each : (r + 1) * each]
    out[...] = block[...].astype(bf16)


def finish(got, out):
    n = got.shape[0]
    parts = got[...].astype(f32)
    flat = parts.reshape(n * 8, WIDTH)
    lane = iota(flat.shape, 1)
    ones = jnp.ones((WIDTH, WIDTH), bf16)
    peaks = dot(jnp.where(lane == 0, flat, 0.0).astype(bf16), ones).reshape(n, 8, WIDTH)
    totals = jnp.where((lane == 1) | (lane == 2), flat, 0.0).astype(bf16)
    totals = dot(totals, ones).reshape(n, 8, WIDTH)
    factors = jnp.exp(peaks - jnp.max(peaks, axis=0)[None]) * totals
    factors = pltpu.roll(factors, ROWS, 1)
    mean = jnp.sum(factors * parts, axis=0) / jnp.sum(factors, axis=0)
    out[...] = jnp.broadcast_to(mean[:ROWS].astype(bf16)[None], out.shape)


def project(attended, weight, out):
    rows = jnp.concatenate([attended[:, r, :].astype(f32) for r in range(ROWS)], axis=0)
    shape = (GROUP * COUNT, GROUP * COUNT)
    to, of = iota(shape, 0), iota(shape, 1)
    move = (to // COUNT == (of // STEPS) % GROUP) & (to % ROWS == of // (GROUP * STEPS))
    move = move & ((to // ROWS) % STEPS == of % STEPS)
    moved = dot(jnp.where(move, 1.0, 0.0).astype(bf16), rows.astype(bf16)).astype(bf16)
    features = jnp.concatenate(
        [moved[COUNT * g : COUNT * (g + 1), :] for g in range(GROUP)], axis=1
    )
    out[...] = jnp.broadcast_to(dot(features, weight[...]).astype(bf16)[None], out.shape)


def normalise(parts, stream_in, gain, core, out, stream_out, rows):
    for i in range(STEPS):
        rows[ROWS * i : ROWS * (i + 1), :] = stream_in[i]
    stream = rows[...] + jnp.sum(parts[...].astype(f32), axis=0)
    for i in range(STEPS):
        stream_out[i] = stream[ROWS * i : ROWS * (i + 1)]
    first = core[0] == 0
    scaled = stream * gain[...]
    scaled = jnp.where(first, scaled[:, :WIDTH], scaled[:, WIDTH:])
    stream = jnp.where(first, stream[:, :WIDTH], stream[:, WIDTH:])
    squares = jnp.sum(stream * stream, axis=1, keepdims=True)
    hi, rest = split(squares)
    mid, rest = split(rest)
    at = iota((COUNT, WIDTH), 1) - iota((COUNT, WIDTH), 0)
    stat = jnp.where(at == 0, hi, jnp.where(at == 32, mid, jnp.where(at == 64, rest, 0.0)))
    stat = jnp.broadcast_to(jnp.sum(stat, axis=0, keepdims=True), (8, WIDTH))
    block = jnp.concatenate([scaled, stat], axis=0).astype(bf16)
    out[...] = jnp.broadcast_to(block[None], out.shape)


def lay(own, other, core, tokens, inverse):
    n = own.shape[0]

    def place(halves):
        for s in range(n):
            for j, half in enumerate(halves):
                at = (2 * s + j) * WIDTH
                tokens[:, at : at + WIDTH] = half[s, :COUNT, :]

    @pl.when(core[0] == 0)
    def _():
        place((own, other))

    @pl.when(core[0] != 0)
    def _():
        place((other, own))

    stats = jnp.sum(own[:, COUNT:, :].astype(f32), axis=0)
    stats = stats + jnp.sum(other[:, COUNT:, :].astype(f32), axis=0)
    stats = jnp.concatenate([stats, stats], axis=0)
    at = iota((COUNT, WIDTH), 1) - iota((COUNT, WIDTH), 0)
    stats = jnp.where((at == 0) | (at == 32) | (at == 64), stats, 0.0)
    squares = jnp.sum(stats, axis=1, keepdims=True)
    inverse[...] = jnp.broadcast_to(
        lax.rsqrt(squares / (n * 2 * WIDTH) + epsilon), inverse.shape
    )


def send(x, axis):
    return lax.all_to_all(x, axis, split_axis=0, concat_axis=0, tiled=True)


def shards(
    queries,
    drafted_key_value,
    paged_key_value,
    block_table,
    page_count,
    tail_fill,
    out_weight,
    stream_in,
    norm_gain,
    gate_up,
):
    seq_index = lax.axis_index(("z", "y"))
    seq_count = lax.axis_size(("z", "y"))
    pages, page_len = paged_key_value.shape[2], paged_key_value.shape[3]
    columns = out_weight.shape[1]
    units = gate_up.shape[1]

    shape = jax.ShapeDtypeStruct
    mine = call(copies, shape((seq_count, STEPS, ROWS * QUARTER), bf16), "v")(queries)
    gathered = send(mine, ("z", "y"))

    drafted = drafted_key_value.transpose(0, 1, 3, 2, 4).reshape(COUNT, 2, WIDTH)
    index = seq_index.reshape(1)
    core = lax.axis_index("core").reshape(1)
    bias, fresh_keys, fresh_values = call(
        prepare,
        (
            shape((ROWS, pages * page_len), f32),
            shape((COUNT, WIDTH), bf16),
            shape((COUNT, WIDTH), bf16),
        ),
        "vsssv",
        limit=8 * 2**20,
    )(block_table, page_count, tail_fill, index, drafted)
    block = call(
        attend,
        shape((seq_count, 2 * ROWS, WIDTH), bf16),
        "vvvvvs",
        [pltpu.VMEM((seq_count, 2 * ROWS, WIDTH), f32)],
    )(gathered, paged_key_value, fresh_keys, fresh_values, bias, index)
    attended = call(finish, shape((seq_count, ROWS, WIDTH), bf16), "v")(
        send(block, ("z", "y"))
    )
    partial_sum = call(project, shape((SIDE, COUNT, columns), bf16), "vv")(
        send(attended, ("z", "y")), out_weight
    )
    scaled, stream = call(
        normalise,
        (shape((seq_count, COUNT + 8, WIDTH), bf16), shape((STEPS, ROWS, columns), f32)),
        "vvvs",
        [pltpu.VMEM((COUNT, columns), f32)],
    )(send(partial_sum, ("x", "core")), stream_in, norm_gain.reshape(1, columns), core)
    own = send(scaled, ("z", "y"))
    other = lax.ppermute(own, "core", [(0, 1), (1, 0)])
    tokens, inverse = call(
        lay,
        (shape((COUNT, seq_count * columns), bf16), shape((COUNT, WIDTH), f32)),
        "vvs",
    )(own, other, core)
    both = jnp.einsum("nc,kfc->knf", tokens, gate_up, preferred_element_type=f32)
    both = both * inverse[None, :, :units]
    hidden = both[0] / (1.0 + jnp.exp(-both[0])) * both[1]
    hidden = hidden.astype(bf16).reshape(STEPS, ROWS, units)
    return hidden, stream


def solution(mesh):
    fine = Mesh(mesh.devices.reshape(4, 2, 8, 8), ("x", "core", "z", "y"))
    kvh, seq = ("x", "core"), ("z", "y")
    placed = (
        P(None, None, kvh + seq),
        P(None, None, None, kvh, None),
        P(None, kvh, seq, None, None),
        P(),
        P(),
        P(),
        P(kvh, seq),
        P(None, None, seq),
        P(seq),
        P(None, kvh + seq, None),
    )
    return jax.shard_map(
        shards,
        mesh=fine,
        in_specs=placed,
        out_specs=(P(None, None, kvh + seq), P(None, None, seq)),
        check_vma=False,
    )
```
